32 devices in a mesh: sect: 2 (over core), tmpl: 16 (over z, y, x).
Axes of the slice: x: 2, y: 2, z: 4, core: 2. Of those that a mesh axis runs over, the one named last changes fastest.
Arguments:
- strain: bfloat16 [2, 1535], P('sect'), may hold values from -6 to 6
- filters: bfloat16 [2, 1024, 1024], P('sect', 'tmpl'), may hold values from -0.1875 to 0.1875
- synthesis: bfloat16 [2, 32768, 1024], P('sect', 'tmpl'), may hold values from -0.1875 to 0.1875
- correlation: float32 [16384, 2, 351], P('tmpl'), may hold values from -0.6 to 0.6
Outputs:
- snr: bfloat16 [32768, 512], P('tmpl', 'sect')
- residual: float32 [16384, 512], P('tmpl', 'sect')
The draws below stay inside these ranges and needn't reach their ends.
All inputs are finite; a program needn't handle non-finite values.
Results may differ from the reference program's by a relative error of at most 0.0049.
Values may be sent and summed in bfloat16 or wider, within the bound.
A program may use at most 128 MiB of HBM per device.

```python
import jax
import jax.numpy as jnp
from jax import lax

TEMPLATES = 16384
BASES = 1024
TAPS = 1024
ACL = 351
KMAX = 4
SAMPLES = 512
SECTIONS = 2
COLUMNS = 32768
DATA_LEN = 1535


def steps_of(own_key, dims, pieces, low, largest):
    def one(dim, shards_of):
        draws = jax.random.uniform(jax.random.fold_in(jax.random.fold_in(own_key, 6), dim), (shards_of,), jnp.float32, low / len(pieces), largest / len(pieces))
        return jnp.repeat(jnp.exp(draws), dims[dim] // shards_of).reshape((-1,) + (1,) * (len(dims) - dim - 1))

    gain = one(*pieces[0])
    for cut in pieces[1:]:
        gain = gain * one(*cut)
    return gain


def scatter_about(rng, dims, deviation, most, split=(), kind=jnp.bfloat16):
    entries = jax.random.normal(rng, dims, jnp.float32) * deviation
    if len(split) > 0:
        entries = steps_of(rng, dims, split, -0.22, 0.18) * entries
    return jnp.clip(entries, min=-most, max=most).astype(kind)


def setup_inputs(seed: int = 0) -> dict:
    streams_of = jax.random.split(jax.random.key(seed), 5)
    return {
        "strain": scatter_about(streams_of[0], (SECTIONS, DATA_LEN), 1.0, 6.0, ((0, 2),)),
        "filters": scatter_about(streams_of[1], (SECTIONS, BASES, TAPS), TAPS ** -0.5, 0.1875, ((0, 2), (1, 16))),
        "synthesis": scatter_about(streams_of[2], (SECTIONS, COLUMNS, BASES), BASES ** -0.5, 0.1875, ((0, 2), (1, 16))),
        "correlation": scatter_about(streams_of[3], (TEMPLATES, 2, ACL), 0.1, 0.6, ((0, 16),), jnp.float32),
    }


def residual_terms(window, centre, correlation):
    groups = correlation.shape[0]
    length = correlation.shape[2]
    real_part = correlation[:, 0, :]
    imag_part = correlation[:, 1, :]
    first = jnp.stack([real_part, imag_part], axis=1)
    second = jnp.stack([imag_part, -real_part], axis=1)
    kernel = jnp.stack([first, second], axis=1).reshape(2 * groups, 2, length)
    products = lax.conv_general_dilated(window[None], kernel, (1,), "VALID", dimension_numbers=("NCH", "OIH", "NCH"), feature_group_count=groups, precision=lax.Precision.HIGHEST)[0]
    outlen = centre.shape[1]
    products = products.reshape(groups, 2, outlen)
    framed = window.reshape(groups, 2, window.shape[1])
    power = framed[:, 0] * framed[:, 0] + framed[:, 1] * framed[:, 1]
    energy = lax.reduce_window(power, jnp.float32(0.0), lax.add, (1, length), (1, 1), "VALID")
    middle = centre.reshape(groups, 2, outlen)
    weight = jnp.sum(real_part * real_part + imag_part * imag_part, axis=1)[:, None]
    cross = middle[:, 0] * products[:, 0] - middle[:, 1] * products[:, 1]
    magnitude = middle[:, 0] * middle[:, 0] + middle[:, 1] * middle[:, 1]
    return (energy - 2.0 * cross + magnitude * weight) / (2.0 * length)


def reference(strain, filters, synthesis, correlation):
    accum = None
    for section in range(SECTIONS):
        divisor_log = min(SECTIONS - 1 - section, KMAX)
        count = SAMPLES >> divisor_log
        signal = strain[section, : count + TAPS - 1]
        basis = lax.conv_general_dilated(signal[None, None, :], filters[section][:, None, :], (1,), "VALID", dimension_numbers=("NCH", "OIH", "NCH"), preferred_element_type=jnp.float32)[0].astype(jnp.bfloat16)
        partial_value = jnp.dot(synthesis[section], basis, preferred_element_type=jnp.float32)
        if accum is None:
            accum = partial_value
        else:
            factor = count // accum.shape[1]
            accum = jnp.repeat(accum, factor, axis=1) + partial_value
    half = (ACL - 1) // 2
    padded = jnp.pad(accum, ((0, 0), (half, half)))
    groups = min(TEMPLATES, 256)
    blocks = TEMPLATES // groups
    windows = padded.reshape(blocks, 2 * groups, padded.shape[1])
    centres = accum.reshape(blocks, 2 * groups, SAMPLES)
    series = correlation.reshape(blocks, groups, 2, ACL)
    residual = lax.map(lambda item: residual_terms(item[0], item[1], item[2]), (windows, centres, series))
    return accum.astype(jnp.bfloat16), residual.reshape(TEMPLATES, SAMPLES)
```

```python
import numpy as np
import jax
import jax.numpy as jnp
from jax import lax
from jax.sharding import PartitionSpec as P

KMAX = 4
LANES = 128


def transforms(samples, share, sections, length):
    centre = (length - 1) // 2
    freqs = -(-(share + length - 1) // (2 * LANES)) * LANES
    omega = np.pi * (np.arange(freqs) + 0.5) / freqs
    times = np.arange(samples)
    angle = times[:, None] * omega[None, :]
    forward = np.concatenate([np.cos(angle), np.sin(angle)], axis=1)
    first = np.arange(sections)[:, None] * share
    near = (times[None] >= first - centre) & (times[None] < first + share + length - 1 - centre)
    forward = np.where(near[:, :, None], forward[None], 0.0)
    lags = (np.arange(length) - centre)[:, None] * omega[None, :]
    series = np.concatenate([np.cos(lags), np.sin(lags)], axis=1)
    back = angle.reshape(sections, share, freqs).transpose(0, 2, 1)
    inverse = np.concatenate([np.cos(back), -np.sin(back)], axis=1) / (2 * freqs)
    reach = times[None, :, None] - (first + np.arange(share)[None])[:, None, :]
    band = (reach >= -centre) & (reach < length - centre)
    return tuple(jnp.asarray(x, jnp.bfloat16) for x in (forward, series, inverse, band))


def dot(a, b):
    return jnp.dot(a, b, preferred_element_type=jnp.float32)


def filtered(signal, bank):
    taps = bank.shape[1]
    samples = signal.shape[0] - taps + 1
    rows = 2 * LANES
    padded = jnp.pad(signal, (0, -signal.shape[0] % LANES))
    width = padded.shape[0] + 1
    shifted = jnp.tile(padded, rows + 1)[: rows * width].reshape(rows, width)
    parts = [
        dot(bank[:, at : at + rows], shifted[:, at : at + samples])
        for at in range(0, taps, rows)
    ]
    return sum(parts[1:], parts[0])


def local(strain, filters, synthesis, correlation):
    sections = lax.axis_size("sect")
    section = lax.axis_index("sect")
    taps = filters.shape[2]
    samples = strain.shape[1] - taps + 1
    share = samples // sections
    length = correlation.shape[2]
    forward, series, inverse, band = transforms(samples, share, sections, length)
    freqs = series.shape[1] // 2
    forward, inverse, band = forward[section], inverse[section], band[section]
    basis = filtered(strain[0], filters[0]).astype(jnp.bfloat16)
    piece = lax.all_gather(basis, "tmpl", axis=0, tiled=True)
    held = jnp.repeat(piece[:, : samples // 2], 2, axis=1)
    piece = jnp.where(section == 0, held, piece)
    own = dot(synthesis[0], piece)
    other = lax.ppermute(own, "sect", [(0, 1), (1, 0)])
    snr = own + other
    a, b = correlation[:, 0, :], correlation[:, 1, :]
    weight = jnp.sum(a * a + b * b, axis=1)[:, None]
    at = dot(a.astype(jnp.bfloat16), series)
    bt = dot(b.astype(jnp.bfloat16), series)
    ac, as_, bc, bs = at[:, :freqs], at[:, freqs:], bt[:, :freqs], bt[:, freqs:]
    pr, pi, mr, mi = ac + bs, as_ - bc, ac - bs, as_ + bc
    pairs = snr.reshape(snr.shape[0] // 2, 2, samples)
    x, y = pairs[:, 0], pairs[:, 1]
    xt = dot(x.astype(jnp.bfloat16), forward)
    yt = dot(y.astype(jnp.bfloat16), forward)
    xc, xs, yc, ys = xt[:, :freqs], xt[:, freqs:], yt[:, :freqs], yt[:, freqs:]
    zpr, zpi, zmr, zmi = xc + ys, yc - xs, xc - ys, -xs - yc
    wpr, wpi = zpr * pr - zpi * pi, zpr * pi + zpi * pr
    wmr, wmi = zmr * mr - zmi * mi, zmr * mi + zmi * mr
    u = jnp.concatenate([wpr + wmr, wpi + wmi], axis=1).astype(jnp.bfloat16)
    v = jnp.concatenate([wpi - wmi, wmr - wpr], axis=1).astype(jnp.bfloat16)
    u = dot(u, inverse)
    v = dot(v, inverse)
    power = x * x + y * y
    high = power.astype(jnp.bfloat16)
    low = (power - high.astype(jnp.float32)).astype(jnp.bfloat16)
    energy = dot(high, band) + dot(low, band)
    centre = lax.dynamic_slice_in_dim(snr, section * share, share, 1)
    mid = centre.reshape(pairs.shape[0], 2, share)
    xm, ym = mid[:, 0], mid[:, 1]
    cross = xm * u + ym * v
    residual = (energy - 2.0 * cross + (xm * xm + ym * ym) * weight) / (2.0 * length)
    return centre.astype(jnp.bfloat16), residual


def solution(mesh):
    placed = (
        P("sect", None),
        P("sect", "tmpl", None),
        P("sect", "tmpl", None),
        P("tmpl", None, None),
    )
    return jax.shard_map(
        local,
        mesh=mesh,
        in_specs=placed,
        out_specs=(P("tmpl", "sect"), P("tmpl", "sect")),
        check_vma=False,
    )
```

```python
import functools

import numpy as np
import jax
import jax.numpy as jnp
from jax import lax
from jax.experimental import pallas as pl
from jax.experimental.pallas import tpu as pltpu
from jax.sharding import PartitionSpec as P

LANES = 128
TAP_GROUP = 256
CHUNK = 256
MESH = pl.DeviceIdType.MESH


def transforms(samples, share, sections, length):
    centre = (length - 1) // 2
    freqs = -(-(share + length - 1) // (2 * LANES)) * LANES
    depth = -(-length // LANES) * LANES
    omega = np.pi * (np.arange(freqs) + 0.5) / freqs
    times = np.arange(samples)
    angle = times[:, None] * omega[None, :]
    forward = np.concatenate([np.cos(angle), np.sin(angle)], axis=1)
    first = np.arange(sections)[:, None] * share
    near = (times[None] >= first - centre) & (times[None] < first + share + length - 1 - centre)
    forward = np.where(near[:, :, None], forward[None], 0.0)
    lags = (np.arange(depth) - centre)[:, None] * omega[None, :]
    series = np.concatenate([np.cos(lags), np.sin(lags)], axis=1)
    series = np.where(np.arange(depth)[:, None] < length, series, 0.0)
    back = angle.reshape(sections, share, freqs).transpose(0, 2, 1)
    inverse = np.concatenate([np.cos(back), -np.sin(back)], axis=1) / (2 * freqs)
    reach = times[None, :, None] - (first + np.arange(share)[None])[:, None, :]
    band = (reach >= -centre) & (reach < length - centre)
    return tuple(np.asarray(x, jnp.bfloat16) for x in (forward, series, inverse, band))


def dot(a, b):
    return jnp.dot(a, b, preferred_element_type=jnp.float32)


def kernel(
    length,
    strain_ref, filters_ref, synthesis_hbm, lags_hbm, weight_ref,
    forward_hbm, series_hbm, inverse_hbm, band_hbm,
    snr_hbm, residual_hbm,
    synthesis, lags, forward, series, inverse, band,
    gathered, own, theirs, spectra, full, turned, snr_out, residual_out,
    in_sems, out_sems, gather_send, gather_recv, swap_send, swap_recv,
):
    n = lax.axis_size("tmpl")
    me = lax.axis_index("tmpl")
    section = lax.axis_index("sect")
    block, samples = filters_ref.shape[0], gathered.shape[1]
    taps = filters_ref.shape[1]
    share = residual_out.shape[1]
    rows = synthesis.shape[0]
    chunks = rows // CHUNK
    half = CHUNK // 2
    tiles = spectra.shape[1]

    loads = [
        pltpu.make_async_copy(src, dst, in_sems.at[i])
        for i, (src, dst) in enumerate([
            (lags_hbm, lags),
            (series_hbm, series),
            (synthesis_hbm.at[0], synthesis),
            (forward_hbm.at[section], forward),
            (inverse_hbm.at[section], inverse),
            (band_hbm.at[section], band),
        ])
    ]
    for load in loads:
        load.start()

    barrier = pltpu.get_barrier_semaphore()

    def greet(step, carry):
        pl.semaphore_signal(
            barrier, inc=1, device_id={"tmpl": lax.rem(me + step, n)}, device_id_type=MESH
        )
        return carry

    lax.fori_loop(1, n, greet, 0)
    pl.semaphore_signal(barrier, inc=1, device_id={"sect": 1 - section}, device_id_type=MESH)

    wide = jnp.broadcast_to(strain_ref[...], (TAP_GROUP, strain_ref.shape[1]))
    width = wide.shape[1]
    hankel = pltpu.roll(wide, width - (TAP_GROUP - 1), 1, stride=1, stride_axis=0)
    hankel = hankel.astype(jnp.bfloat16)
    down = lax.broadcasted_iota(jnp.int32, (TAP_GROUP, TAP_GROUP), 0)
    across = lax.broadcasted_iota(jnp.int32, (TAP_GROUP, TAP_GROUP), 1)
    flip = jnp.where(down + across == TAP_GROUP - 1, 1.0, 0.0).astype(jnp.bfloat16)
    basis = jnp.zeros((block, samples), jnp.float32)
    for at in range(0, taps, TAP_GROUP):
        bank = dot(filters_ref[:, at : at + TAP_GROUP], flip).astype(jnp.bfloat16)
        basis = basis + dot(bank, hankel[:, at : at + samples])
    source = lax.broadcasted_iota(jnp.int32, (samples, samples), 0)
    target = lax.broadcasted_iota(jnp.int32, (samples, samples), 1)
    target = jnp.where(section == 0, target >> 1, target)
    hold = jnp.where(source == target, 1.0, 0.0).astype(jnp.bfloat16)
    mine = gathered.at[pl.ds(pl.multiple_of(me * block, block), block)]
    mine[...] = dot(basis.astype(jnp.bfloat16), hold).astype(jnp.bfloat16)

    pl.semaphore_wait(barrier, n)

    def push(step):
        return pltpu.make_async_remote_copy(
            src_ref=mine,
            dst_ref=mine,
            send_sem=gather_send.at[step],
            recv_sem=gather_recv.at[step],
            device_id={"tmpl": lax.rem(me + step, n)},
            device_id_type=MESH,
        )

    def start_push(step, carry):
        push(step).start()
        return carry

    def wait_push(step, carry):
        push(step).wait()
        return carry

    lax.fori_loop(1, n, start_push, 0)

    loads[0].wait()
    loads[1].wait()

    def analyse(c, carry):
        at = pl.ds(pl.multiple_of(c * half, half), half)
        real = dot(lags[0, at, :], series[...])
        imag = dot(lags[1, at, :], series[...])
        for i in range(tiles):
            cos = slice(i * LANES, (i + 1) * LANES)
            sin = slice((tiles + i) * LANES, (tiles + i + 1) * LANES)
            ac, as_, bc, bs = real[:, cos], real[:, sin], imag[:, cos], imag[:, sin]
            spectra[0, i, at, :] = ac + bs
            spectra[1, i, at, :] = as_ - bc
            spectra[2, i, at, :] = ac - bs
            spectra[3, i, at, :] = as_ + bc
        return carry

    lax.fori_loop(0, chunks, analyse, 0)
    for load in loads[2:]:
        load.wait()
    lax.fori_loop(1, n, wait_push, 0)

    def swap(c):
        at = pl.ds(pl.multiple_of(c * CHUNK, CHUNK), CHUNK)
        return pltpu.make_async_remote_copy(
            src_ref=own.at[at],
            dst_ref=theirs.at[at],
            send_sem=swap_send.at[c],
            recv_sem=swap_recv.at[c],
            device_id={"sect": 1 - section},
            device_id_type=MESH,
        )

    def reconstruct(c, carry):
        at = pl.ds(pl.multiple_of(c * CHUNK, CHUNK), CHUNK)
        value = dot(synthesis[at, :], gathered[...])
        own[at, :] = value.astype(jnp.bfloat16)
        swap(c).start()
        for i in range(samples // LANES):
            full[i, at, :] = value[:, i * LANES : (i + 1) * LANES]
        return carry

    lax.fori_loop(0, chunks, reconstruct, 0)

    def emit(c):
        at = pl.ds(pl.multiple_of(c * CHUNK, CHUNK), CHUNK)
        to = pl.ds(pl.multiple_of(c * half, half), half)
        return (
            pltpu.make_async_copy(snr_out.at[at], snr_hbm.at[at], out_sems.at[0, c]),
            pltpu.make_async_copy(residual_out.at[to], residual_hbm.at[to], out_sems.at[1, c]),
        )

    def resolve(c, carry):
        start = pl.multiple_of(c * CHUNK, CHUNK)
        at = pl.ds(start, CHUNK)
        to = pl.ds(pl.multiple_of(c * half, half), half)
        even = pl.ds(start, half, stride=2)
        odd = pl.ds(start + 1, half, stride=2)
        swap(c).wait()
        parts = []
        for i in range(samples // LANES):
            part = full[i, at, :] + theirs[at, i * LANES : (i + 1) * LANES].astype(jnp.float32)
            full[i, at, :] = part
            parts.append(part.astype(jnp.bfloat16))
        spectrum = dot(jnp.concatenate(parts, axis=1), forward[...])
        for i in range(2 * tiles):
            turned[i] = spectrum[:, i * LANES : (i + 1) * LANES]
        evens, odds = pl.ds(0, half, stride=2), pl.ds(1, half, stride=2)
        ur, ui, vr, vi = [], [], [], []
        for i in range(tiles):
            xc, yc = turned[i, evens, :], turned[i, odds, :]
            xs, ys = turned[tiles + i, evens, :], turned[tiles + i, odds, :]
            pr, pi = spectra[0, i, to, :], spectra[1, i, to, :]
            mr, mi = spectra[2, i, to, :], spectra[3, i, to, :]
            zpr, zpi, zmr, zmi = xc + ys, yc - xs, xc - ys, -xs - yc
            wpr, wpi = zpr * pr - zpi * pi, zpr * pi + zpi * pr
            wmr, wmi = zmr * mr - zmi * mi, zmr * mi + zmi * mr
            ur.append((wpr + wmr).astype(jnp.bfloat16))
            ui.append((wpi + wmi).astype(jnp.bfloat16))
            vr.append((wpi - wmi).astype(jnp.bfloat16))
            vi.append((wmr - wpr).astype(jnp.bfloat16))
        u = dot(jnp.concatenate(ur + ui, axis=1), inverse[...])
        v = dot(jnp.concatenate(vr + vi, axis=1), inverse[...])
        high, low = [], []
        for i in range(samples // LANES):
            x, y = full[i, even, :], full[i, odd, :]
            power = x * x + y * y
            top = power.astype(jnp.bfloat16)
            high.append(top)
            low.append((power - top.astype(jnp.float32)).astype(jnp.bfloat16))
        energy = dot(jnp.concatenate(high, axis=1), band[...])
        energy = energy + dot(jnp.concatenate(low, axis=1), band[...])
        weight = weight_ref[to, :]
        for i in range(share // LANES):
            columns = slice(i * LANES, (i + 1) * LANES)
            tile = section * (share // LANES) + i
            snr_out[at, columns] = full[tile, at, :].astype(jnp.bfloat16)
            x, y = full[tile, even, :], full[tile, odd, :]
            cross = x * u[:, columns] + y * v[:, columns]
            value = energy[:, columns] - 2.0 * cross + (x * x + y * y) * weight
            residual_out[to, columns] = value / (2.0 * length)
        for copy in emit(c):
            copy.start()
        return carry

    lax.fori_loop(0, chunks, resolve, 0)

    def finish(c, carry):
        for copy in emit(c):
            copy.wait()
        return carry

    lax.fori_loop(0, chunks, finish, 0)


def local(strain, filters, synthesis, correlation):
    sections = lax.axis_size("sect")
    n = lax.axis_size("tmpl")
    block, taps = filters.shape[1:]
    samples = strain.shape[1] - taps + 1
    share = samples // sections
    rows = synthesis.shape[1]
    groups, _, length = correlation.shape
    forward, series, inverse, band = transforms(samples, share, sections, length)
    depth, spectrum = series.shape
    tiles = spectrum // (2 * LANES)
    chunks = rows // CHUNK
    signal = jnp.pad(strain, ((0, 0), (0, -strain.shape[1] % LANES))).astype(jnp.float32)
    lags = jnp.pad(correlation, ((0, 0), (0, 0), (0, depth - length))).transpose(1, 0, 2)
    weight = jnp.sum(correlation * correlation, axis=(1, 2))[:, None]
    vmem = pl.BlockSpec(memory_space=pltpu.VMEM)
    hbm = pl.BlockSpec(memory_space=pl.ANY)
    return pl.pallas_call(
        functools.partial(kernel, length),
        out_shape=(
            jax.ShapeDtypeStruct((rows, share), jnp.bfloat16),
            jax.ShapeDtypeStruct((groups, share), jnp.float32),
        ),
        in_specs=[vmem, vmem, hbm, hbm, vmem, hbm, hbm, hbm, hbm],
        out_specs=(hbm, hbm),
        scratch_shapes=[
            pltpu.VMEM((rows, n * block), jnp.bfloat16),
            pltpu.VMEM((2, groups, depth), jnp.bfloat16),
            pltpu.VMEM(forward.shape[1:], jnp.bfloat16),
            pltpu.VMEM(series.shape, jnp.bfloat16),
            pltpu.VMEM(inverse.shape[1:], jnp.bfloat16),
            pltpu.VMEM(band.shape[1:], jnp.bfloat16),
            pltpu.VMEM((n * block, samples), jnp.bfloat16),
            pltpu.VMEM((rows, samples), jnp.bfloat16),
            pltpu.VMEM((rows, samples), jnp.bfloat16),
            pltpu.VMEM((4, tiles, groups, LANES), jnp.float32),
            pltpu.VMEM((samples // LANES, rows, LANES), jnp.float32),
            pltpu.VMEM((2 * tiles, CHUNK, LANES), jnp.float32),
            pltpu.VMEM((rows, share), jnp.bfloat16),
            pltpu.VMEM((groups, share), jnp.float32),
            pltpu.SemaphoreType.DMA((6,)),
            pltpu.SemaphoreType.DMA((2, chunks)),
            pltpu.SemaphoreType.DMA((n,)),
            pltpu.SemaphoreType.DMA((n,)),
            pltpu.SemaphoreType.DMA((chunks,)),
            pltpu.SemaphoreType.DMA((chunks,)),
        ],
        compiler_params=pltpu.CompilerParams(
            collective_id=0, has_side_effects=True, vmem_limit_bytes=56 * 2**20
        ),
    )(
        signal, filters[0], synthesis, lags.astype(jnp.bfloat16), weight,
        forward, series, inverse, band,
    )


def solution(mesh):
    placed = (
        P("sect", None),
        P("sect", "tmpl", None),
        P("sect", "tmpl", None),
        P("tmpl", None, None),
    )
    return jax.shard_map(
        local,
        mesh=mesh,
        in_specs=placed,
        out_specs=(P("tmpl", "sect"), P("tmpl", "sect")),
        check_vma=False,
    )
```

```python
import functools

import numpy as np
import jax
import jax.numpy as jnp
from jax import lax
from jax.experimental import pallas as pl
from jax.experimental.pallas import tpu as pltpu
from jax.sharding import PartitionSpec as P

LANES = 128
TAP_GROUP = 256
CHUNK = 256
MESH = pl.DeviceIdType.MESH


def transforms(samples, share, sections, length):
    centre = (length - 1) // 2
    freqs = -(-(share + length - 1) // (2 * LANES)) * LANES
    depth = -(-length // LANES) * LANES
    omega = np.pi * (np.arange(freqs) + 0.5) / freqs
    times = np.arange(samples)
    angle = times[:, None] * omega[None, :]
    forward = np.concatenate([np.cos(angle), np.sin(angle)], axis=1)
    first = np.arange(sections)[:, None] * share
    near = (times[None] >= first - centre) & (times[None] < first + share + length - 1 - centre)
    forward = np.where(near[:, :, None], forward[None], 0.0)
    lags = (np.arange(depth) - centre)[:, None] * omega[None, :]
    series = np.concatenate([np.cos(lags), np.sin(lags)], axis=1)
    series = np.where(np.arange(depth)[:, None] < length, series, 0.0)
    back = angle.reshape(sections, share, freqs).transpose(0, 2, 1)
    inverse = np.concatenate([np.cos(back), -np.sin(back)], axis=1) / (2 * freqs)
    reach = times[None, :, None] - (first + np.arange(share)[None])[:, None, :]
    band = (reach >= -centre) & (reach < length - centre)
    return tuple(np.asarray(x, jnp.bfloat16) for x in (forward, series, inverse, band))


def dot(a, b):
    return jnp.dot(a, b, preferred_element_type=jnp.float32)


def dot_rows(a, b):
    return lax.dot_general(a, b, (((0,), (0,)), ((), ())), preferred_element_type=jnp.float32)


def kernel(
    length, grid,
    strain_ref, filters_ref, synthesis_hbm, lags_hbm,
    forward_hbm, series_hbm, inverse_hbm, band_hbm,
    snr_hbm, residual_hbm,
    synthesis, lags, forward, series, inverse, band,
    gathered, own, theirs, spectra, weights, full, turned, snr_out, residual_out,
    in_sems, out_sems, line_send, line_recv, relay_send, relay_recv, swap_send, swap_recv,
):
    n = lax.axis_size("tmpl")
    me = lax.axis_index("tmpl")
    section = lax.axis_index("sect")
    block, samples = filters_ref.shape[0], gathered.shape[1]
    taps = filters_ref.shape[1]
    share = residual_out.shape[1]
    rows = synthesis.shape[0]
    chunks = rows // CHUNK
    half = CHUNK // 2
    tiles = spectra.shape[1]

    loads = [
        pltpu.make_async_copy(src, dst, in_sems.at[i])
        for i, (src, dst) in enumerate([
            (lags_hbm, lags.at[pl.ds(0, length)]),
            (series_hbm, series),
            (synthesis_hbm.at[0], synthesis),
            (forward_hbm.at[section], forward),
            (inverse_hbm.at[section], inverse),
            (band_hbm.at[section], band),
        ])
    ]
    for load in loads:
        load.start()

    depth, height, breadth = grid
    place = (me // (height * breadth), me // breadth % height, me % breadth)

    def toward(axis, step):
        where = [lax.rem(p + step, size) if i == axis else p for i, (p, size) in enumerate(zip(place, grid))]
        return {"tmpl": (where[0] * height + where[1]) * breadth + where[2]}

    barrier = pltpu.get_barrier_semaphore()
    for axis in range(3):
        for step in range(1, grid[axis]):
            pl.semaphore_signal(barrier, inc=1, device_id=toward(axis, step), device_id_type=MESH)
    pl.semaphore_signal(barrier, inc=1, device_id={"sect": 1 - section}, device_id_type=MESH)
    lags[pl.ds(length, lags.shape[0] - length)] = jnp.zeros(
        (lags.shape[0] - length,) + lags.shape[1:], jnp.float32
    )

    signal = strain_ref[...].astype(jnp.float32)
    signal = jnp.concatenate([signal, jnp.zeros((1, -signal.shape[1] % LANES), jnp.float32)], axis=1)
    wide = jnp.broadcast_to(signal, (TAP_GROUP, signal.shape[1]))
    width = wide.shape[1]
    hankel = pltpu.roll(wide, width - (TAP_GROUP - 1), 1, stride=1, stride_axis=0)
    hankel = hankel.astype(jnp.bfloat16)
    down = lax.broadcasted_iota(jnp.int32, (TAP_GROUP, TAP_GROUP), 0)
    across = lax.broadcasted_iota(jnp.int32, (TAP_GROUP, TAP_GROUP), 1)
    flip = jnp.where(down + across == TAP_GROUP - 1, 1.0, 0.0).astype(jnp.bfloat16)
    basis = jnp.zeros((block, samples), jnp.float32)
    for at in range(0, taps, TAP_GROUP):
        bank = dot(filters_ref[:, at : at + TAP_GROUP], flip).astype(jnp.bfloat16)
        basis = basis + dot(bank, hankel[:, at : at + samples])
    mine = gathered.at[pl.ds(pl.multiple_of(me * block, block), block)]
    mine[...] = basis.astype(jnp.bfloat16)

    pl.semaphore_wait(barrier, sum(grid) - 3 + 1)

    def analyse(c, carry):
        at = pl.ds(pl.multiple_of(c * half, half), half)
        a, b = lags[:, 0, at], lags[:, 1, at]
        real = dot_rows(a.astype(jnp.bfloat16), series[...])
        imag = dot_rows(b.astype(jnp.bfloat16), series[...])
        power = a * a + b * b
        high = power.astype(jnp.bfloat16)
        low = (power - high.astype(jnp.float32)).astype(jnp.bfloat16)
        ones = jnp.ones((lags.shape[0], LANES), jnp.bfloat16)
        weights[at, :] = dot_rows(high, ones) + dot_rows(low, ones)
        for i in range(tiles):
            cos = slice(i * LANES, (i + 1) * LANES)
            sin = slice((tiles + i) * LANES, (tiles + i + 1) * LANES)
            ac, as_, bc, bs = real[:, cos], real[:, sin], imag[:, cos], imag[:, sin]
            spectra[0, i, at, :] = ac + bs
            spectra[1, i, at, :] = as_ - bc
            spectra[2, i, at, :] = ac - bs
            spectra[3, i, at, :] = as_ + bc
        return carry

    def gather(used):
        whole = pl.ds(0, used)
        parts = (pl.ds(0, used // 2), pl.ds(used // 2, used // 2))

        def spot(offset, columns):
            where = [lax.rem(p - o + size, size) for p, o, size in zip(place, offset, grid)]
            index = (where[0] * height + where[1]) * breadth + where[2]
            return gathered.at[pl.ds(pl.multiple_of(index * block, block), block), columns]

        def line(step):
            here = spot((0, 0, 0), whole)
            return pltpu.make_async_remote_copy(
                src_ref=here, dst_ref=here, send_sem=line_send.at[step], recv_sem=line_recv.at[step],
                device_id=toward(0, step), device_id_type=MESH,
            )

        def relay(part, offset, axis, step):
            here = spot(offset, parts[part])
            there = tuple(step if i == axis else o for i, o in enumerate(offset))
            slot = (part,) + there
            return pltpu.make_async_remote_copy(
                src_ref=here, dst_ref=here, send_sem=relay_send.at[slot], recv_sem=relay_recv.at[slot],
                device_id=toward(axis, step), device_id_type=MESH,
            )

        def arrive_line(step):
            here = spot((step, 0, 0), whole)
            pltpu.make_async_remote_copy(
                src_ref=here, dst_ref=here, send_sem=line_send.at[step], recv_sem=line_recv.at[step],
                device_id=toward(0, step), device_id_type=MESH,
            ).wait_recv()

        def arrive(part, offset):
            here = spot(offset, parts[part])
            slot = (part,) + offset
            pltpu.make_async_remote_copy(
                src_ref=here, dst_ref=here, send_sem=relay_send.at[slot], recv_sem=relay_recv.at[slot],
                device_id=toward(0, 1), device_id_type=MESH,
            ).wait_recv()

        sent = []

        def send(copy):
            copy.start()
            sent.append(copy)

        def spread(dz):
            for part in range(2):
                for axis in ((1, 2) if part == 0 else (2, 1)):
                    for step in range(1, grid[axis]):
                        send(relay(part, (dz, 0, 0), axis, step))

        for step in range(1, depth):
            send(line(step))
        spread(0)
        loads[0].wait()
        loads[1].wait()
        lax.fori_loop(0, chunks // 2, analyse, 0)
        for dz in range(1, depth):
            arrive_line(dz)
            spread(dz)
        lax.fori_loop(chunks // 2, chunks * 3 // 4, analyse, 0)
        for dz in range(depth):
            for step in range(1, height):
                arrive(0, (dz, step, 0))
                for last in range(1, breadth):
                    send(relay(0, (dz, step, 0), 2, last))
            for step in range(1, breadth):
                arrive(1, (dz, 0, step))
                for last in range(1, height):
                    send(relay(1, (dz, 0, step), 1, last))
        lax.fori_loop(chunks * 3 // 4, chunks, analyse, 0)
        for dz in range(depth):
            for dy in range(height):
                for dx in range(1, breadth):
                    arrive(0, (dz, dy, dx))
            for dx in range(breadth):
                for dy in range(1, height):
                    arrive(1, (dz, dy, dx))
        for copy in sent:
            copy.wait_send()

    @pl.when(section == 0)
    def _():
        gather(samples // 2)
        source = lax.broadcasted_iota(jnp.int32, (samples // 2, samples), 0)
        target = lax.broadcasted_iota(jnp.int32, (samples // 2, samples), 1)
        hold = jnp.where(source == target // 2, 1.0, 0.0).astype(jnp.bfloat16)
        for at in range(0, gathered.shape[0], 256):
            some = slice(at, at + 256)
            gathered[some, :] = dot(gathered[some, : samples // 2], hold).astype(jnp.bfloat16)

    @pl.when(section != 0)
    def _():
        gather(samples)

    for load in loads[2:]:
        load.wait()

    def swap(c):
        at = pl.ds(pl.multiple_of(c * CHUNK, CHUNK), CHUNK)
        return pltpu.make_async_remote_copy(
            src_ref=own.at[at],
            dst_ref=theirs.at[at],
            send_sem=swap_send.at[c],
            recv_sem=swap_recv.at[c],
            device_id={"sect": 1 - section},
            device_id_type=MESH,
        )

    def reconstruct(c, carry):
        at = pl.ds(pl.multiple_of(c * CHUNK, CHUNK), CHUNK)
        value = dot(synthesis[at, :], gathered[...])
        own[at, :] = value.astype(jnp.bfloat16)
        swap(c).start()
        for i in range(samples // LANES):
            full[i, at, :] = value[:, i * LANES : (i + 1) * LANES]
        return carry

    lax.fori_loop(0, chunks, reconstruct, 0)

    def emit(c):
        at = pl.ds(pl.multiple_of(c * CHUNK, CHUNK), CHUNK)
        to = pl.ds(pl.multiple_of(c * half, half), half)
        return (
            pltpu.make_async_copy(snr_out.at[at], snr_hbm.at[at], out_sems.at[0, c]),
            pltpu.make_async_copy(residual_out.at[to], residual_hbm.at[to], out_sems.at[1, c]),
        )

    def resolve(c, carry):
        start = pl.multiple_of(c * CHUNK, CHUNK)
        at = pl.ds(start, CHUNK)
        to = pl.ds(pl.multiple_of(c * half, half), half)
        even = pl.ds(start, half, stride=2)
        odd = pl.ds(start + 1, half, stride=2)
        swap(c).wait()
        parts = []
        for i in range(samples // LANES):
            part = full[i, at, :] + theirs[at, i * LANES : (i + 1) * LANES].astype(jnp.float32)
            full[i, at, :] = part
            parts.append(part.astype(jnp.bfloat16))
        spectrum = dot(jnp.concatenate(parts, axis=1), forward[...])
        for i in range(2 * tiles):
            turned[i] = spectrum[:, i * LANES : (i + 1) * LANES]
        evens, odds = pl.ds(0, half, stride=2), pl.ds(1, half, stride=2)
        ur, ui, vr, vi = [], [], [], []
        for i in range(tiles):
            xc, yc = turned[i, evens, :], turned[i, odds, :]
            xs, ys = turned[tiles + i, evens, :], turned[tiles + i, odds, :]
            pr, pi = spectra[0, i, to, :], spectra[1, i, to, :]
            mr, mi = spectra[2, i, to, :], spectra[3, i, to, :]
            zpr, zpi, zmr, zmi = xc + ys, yc - xs, xc - ys, -xs - yc
            wpr, wpi = zpr * pr - zpi * pi, zpr * pi + zpi * pr
            wmr, wmi = zmr * mr - zmi * mi, zmr * mi + zmi * mr
            ur.append((wpr + wmr).astype(jnp.bfloat16))
            ui.append((wpi + wmi).astype(jnp.bfloat16))
            vr.append((wpi - wmi).astype(jnp.bfloat16))
            vi.append((wmr - wpr).astype(jnp.bfloat16))
        u = dot(jnp.concatenate(ur + ui, axis=1), inverse[...])
        v = dot(jnp.concatenate(vr + vi, axis=1), inverse[...])
        high, low = [], []
        for i in range(samples // LANES):
            x, y = full[i, even, :], full[i, odd, :]
            power = x * x + y * y
            top = power.astype(jnp.bfloat16)
            high.append(top)
            low.append((power - top.astype(jnp.float32)).astype(jnp.bfloat16))
        energy = dot(jnp.concatenate(high, axis=1), band[...])
        energy = energy + dot(jnp.concatenate(low, axis=1), band[...])
        weight = weights[to, :]
        for i in range(share // LANES):
            columns = slice(i * LANES, (i + 1) * LANES)
            tile = section * (share // LANES) + i
            snr_out[at, columns] = full[tile, at, :].astype(jnp.bfloat16)
            x, y = full[tile, even, :], full[tile, odd, :]
            cross = x * u[:, columns] + y * v[:, columns]
            value = energy[:, columns] - 2.0 * cross + (x * x + y * y) * weight
            residual_out[to, columns] = value / (2.0 * length)
        for copy in emit(c):
            copy.start()
        return carry

    lax.fori_loop(0, chunks, resolve, 0)

    def finish(c, carry):
        for copy in emit(c):
            copy.wait()
        return carry

    lax.fori_loop(0, chunks, finish, 0)


def grid_of(mesh):
    tmpl = mesh.axis_names.index("tmpl")
    line = np.moveaxis(mesh.devices, tmpl, 0).reshape(mesh.shape["tmpl"], -1)[:, 0]
    spots = np.array([device.coords for device in line])[:, ::-1]
    spots = spots - spots.min(axis=0)
    grid = tuple(int(size) for size in spots.max(axis=0) + 1)
    if np.array_equal(spots @ [grid[1] * grid[2], grid[2], 1], np.arange(len(line))):
        return grid
    return (len(line), 1, 1)


def local(grid, strain, filters, synthesis, correlation):
    sections = lax.axis_size("sect")
    n = lax.axis_size("tmpl")
    block, taps = filters.shape[1:]
    samples = strain.shape[1] - taps + 1
    share = samples // sections
    rows = synthesis.shape[1]
    groups, _, length = correlation.shape
    forward, series, inverse, band = transforms(samples, share, sections, length)
    depth, spectrum = series.shape
    tiles = spectrum // (2 * LANES)
    chunks = rows // CHUNK
    vmem = pl.BlockSpec(memory_space=pltpu.VMEM)
    hbm = pl.BlockSpec(memory_space=pl.ANY)
    return pl.pallas_call(
        functools.partial(kernel, length, grid),
        out_shape=(
            jax.ShapeDtypeStruct((rows, share), jnp.bfloat16),
            jax.ShapeDtypeStruct((groups, share), jnp.float32),
        ),
        in_specs=[vmem, vmem, hbm, hbm, hbm, hbm, hbm, hbm],
        out_specs=(hbm, hbm),
        scratch_shapes=[
            pltpu.VMEM((rows, n * block), jnp.bfloat16),
            pltpu.VMEM((depth, 2, groups), jnp.float32),
            pltpu.VMEM(forward.shape[1:], jnp.bfloat16),
            pltpu.VMEM(series.shape, jnp.bfloat16),
            pltpu.VMEM(inverse.shape[1:], jnp.bfloat16),
            pltpu.VMEM(band.shape[1:], jnp.bfloat16),
            pltpu.VMEM((n * block, samples), jnp.bfloat16),
            pltpu.VMEM((rows, samples), jnp.bfloat16),
            pltpu.VMEM((rows, samples), jnp.bfloat16),
            pltpu.VMEM((4, tiles, groups, LANES), jnp.float32),
            pltpu.VMEM((groups, LANES), jnp.float32),
            pltpu.VMEM((samples // LANES, rows, LANES), jnp.float32),
            pltpu.VMEM((2 * tiles, CHUNK, LANES), jnp.float32),
            pltpu.VMEM((rows, share), jnp.bfloat16),
            pltpu.VMEM((groups, share), jnp.float32),
            pltpu.SemaphoreType.DMA((6,)),
            pltpu.SemaphoreType.DMA((2, chunks)),
            pltpu.SemaphoreType.DMA((grid[0],)),
            pltpu.SemaphoreType.DMA((grid[0],)),
            pltpu.SemaphoreType.DMA((2,) + grid),
            pltpu.SemaphoreType.DMA((2,) + grid),
            pltpu.SemaphoreType.DMA((chunks,)),
            pltpu.SemaphoreType.DMA((chunks,)),
        ],
        compiler_params=pltpu.CompilerParams(
            collective_id=0, has_side_effects=True, vmem_limit_bytes=36 * 2**20
        ),
    )(
        strain, filters[0], synthesis, correlation.transpose(2, 1, 0),
        forward, series, inverse, band,
    )


def solution(mesh):
    placed = (
        P("sect", None),
        P("sect", "tmpl", None),
        P("sect", "tmpl", None),
        P("tmpl", None, None),
    )
    return jax.shard_map(
        functools.partial(local, grid_of(mesh)),
        mesh=mesh,
        in_specs=placed,
        out_specs=(P("tmpl", "sect"), P("tmpl", "sect")),
        check_vma=False,
    )
```

```python
import functools

import numpy as np
import jax
import jax.numpy as jnp
from jax import lax
from jax.experimental import pallas as pl
from jax.experimental.pallas import tpu as pltpu
from jax.sharding import PartitionSpec as P

LANES = 128
TAP_GROUP = 256
CHUNK = 256
MESH = pl.DeviceIdType.MESH


def transforms(samples, share, sections, length):
    centre = (length - 1) // 2
    freqs = -(-(share + length - 1) // (2 * LANES)) * LANES
    depth = -(-length // LANES) * LANES
    omega = np.pi * (np.arange(freqs) + 0.5) / freqs
    times = np.arange(samples)
    angle = times[:, None] * omega[None, :]
    forward = np.concatenate([np.cos(angle), np.sin(angle)], axis=1)
    first = np.arange(sections)[:, None] * share
    near = (times[None] >= first - centre) & (times[None] < first + share + length - 1 - centre)
    forward = np.where(near[:, :, None], forward[None], 0.0)
    lags = (np.arange(depth) - centre)[:, None] * omega[None, :]
    series = np.concatenate([np.cos(lags), np.sin(lags)], axis=1)
    series = np.where(np.arange(depth)[:, None] < length, series, 0.0)
    back = angle.reshape(sections, share, freqs).transpose(0, 2, 1)
    inverse = np.concatenate([np.cos(back), -np.sin(back)], axis=1) / (2 * freqs)
    reach = times[None, :, None] - (first + np.arange(share)[None])[:, None, :]
    band = (reach >= -centre) & (reach < length - centre)
    return tuple(np.asarray(x, jnp.bfloat16) for x in (forward, series, inverse, band))


def dot(a, b):
    return jnp.dot(a, b, preferred_element_type=jnp.float32)


def dot_rows(a, b):
    return lax.dot_general(a, b, (((0,), (0,)), ((), ())), preferred_element_type=jnp.float32)


def kernel(
    length, grid,
    strain_hbm, filters_hbm, synthesis_hbm, lags_hbm,
    forward_hbm, series_hbm, inverse_hbm, band_hbm,
    snr_hbm, residual_hbm,
    strain_ref, filters_ref, synthesis, lags, forward, series, inverse, band,
    gathered, own, theirs, spectra, weights, kept, full, snr_out, residual_out,
    in_sems, out_sems, line_send, line_recv, relay_send, relay_recv, swap_send, swap_recv,
):
    n = lax.axis_size("tmpl")
    me = lax.axis_index("tmpl")
    section = lax.axis_index("sect")
    block, samples = filters_ref.shape[0], gathered.shape[1]
    taps = filters_ref.shape[1]
    share = residual_out.shape[1]
    rows = synthesis.shape[0]
    chunks = rows // CHUNK
    half = CHUNK // 2
    tiles = spectra.shape[1]

    loads = [
        pltpu.make_async_copy(src, dst, in_sems.at[i])
        for i, (src, dst) in enumerate([
            (strain_hbm, strain_ref),
            (filters_hbm, filters_ref),
            (lags_hbm, lags.at[pl.ds(0, length)]),
            (series_hbm, series),
            (synthesis_hbm.at[0], synthesis),
            (forward_hbm.at[section], forward),
            (inverse_hbm.at[section], inverse),
            (band_hbm.at[section], band),
        ])
    ]
    for load in loads:
        load.start()

    depth, height, breadth = grid
    place = (me // (height * breadth), me // breadth % height, me % breadth)

    def toward(axis, step):
        where = [lax.rem(p + step, size) if i == axis else p for i, (p, size) in enumerate(zip(place, grid))]
        return {"tmpl": (where[0] * height + where[1]) * breadth + where[2]}

    barrier = pltpu.get_barrier_semaphore()
    for axis in range(3):
        for step in range(1, grid[axis]):
            pl.semaphore_signal(barrier, inc=1, device_id=toward(axis, step), device_id_type=MESH)
    pl.semaphore_signal(barrier, inc=1, device_id={"sect": 1 - section}, device_id_type=MESH)
    lags[pl.ds(length, lags.shape[0] - length)] = jnp.zeros(
        (lags.shape[0] - length,) + lags.shape[1:], jnp.float32
    )

    loads[0].wait()
    loads[1].wait()
    signal = strain_ref[...].astype(jnp.float32)
    signal = jnp.concatenate([signal, jnp.zeros((1, -signal.shape[1] % LANES), jnp.float32)], axis=1)
    wide = jnp.broadcast_to(signal, (TAP_GROUP, signal.shape[1]))
    width = wide.shape[1]
    hankel = pltpu.roll(wide, width - (TAP_GROUP - 1), 1, stride=1, stride_axis=0)
    hankel = hankel.astype(jnp.bfloat16)
    down = lax.broadcasted_iota(jnp.int32, (TAP_GROUP, TAP_GROUP), 0)
    across = lax.broadcasted_iota(jnp.int32, (TAP_GROUP, TAP_GROUP), 1)
    flip = jnp.where(down + across == TAP_GROUP - 1, 1.0, 0.0).astype(jnp.bfloat16)
    basis = jnp.zeros((block, samples), jnp.float32)
    for at in range(0, taps, TAP_GROUP):
        bank = dot(filters_ref[:, at : at + TAP_GROUP], flip).astype(jnp.bfloat16)
        basis = basis + dot(bank, hankel[:, at : at + samples])
    mine = gathered.at[pl.ds(pl.multiple_of(me * block, block), block)]
    mine[...] = basis.astype(jnp.bfloat16)

    pl.semaphore_wait(barrier, sum(grid) - 3 + 1)

    def analyse(c, carry):
        at = pl.ds(pl.multiple_of(c * half, half), half)
        a, b = lags[:, 0, at], lags[:, 1, at]
        real = dot_rows(a.astype(jnp.bfloat16), series[...])
        imag = dot_rows(b.astype(jnp.bfloat16), series[...])
        power = a * a + b * b
        high = power.astype(jnp.bfloat16)
        low = (power - high.astype(jnp.float32)).astype(jnp.bfloat16)
        ones = jnp.ones((lags.shape[0], LANES), jnp.bfloat16)
        weights[at, :] = dot_rows(high, ones) + dot_rows(low, ones)
        for i in range(tiles):
            cos = slice(i * LANES, (i + 1) * LANES)
            sin = slice((tiles + i) * LANES, (tiles + i + 1) * LANES)
            ac, as_, bc, bs = real[:, cos], real[:, sin], imag[:, cos], imag[:, sin]
            spectra[0, i, at, :] = ac + bs
            spectra[1, i, at, :] = as_ - bc
            spectra[2, i, at, :] = ac - bs
            spectra[3, i, at, :] = as_ + bc
        return carry

    def gather(used):
        whole = pl.ds(0, used)
        parts = (pl.ds(0, used // 2), pl.ds(used // 2, used // 2))

        def spot(offset, columns):
            where = [lax.rem(p - o + size, size) for p, o, size in zip(place, offset, grid)]
            index = (where[0] * height + where[1]) * breadth + where[2]
            return gathered.at[pl.ds(pl.multiple_of(index * block, block), block), columns]

        def line(step):
            here = spot((0, 0, 0), whole)
            return pltpu.make_async_remote_copy(
                src_ref=here, dst_ref=here, send_sem=line_send.at[step], recv_sem=line_recv.at[step],
                device_id=toward(0, step), device_id_type=MESH,
            )

        def relay(part, offset, axis, step):
            here = spot(offset, parts[part])
            there = tuple(step if i == axis else o for i, o in enumerate(offset))
            slot = (part,) + there
            return pltpu.make_async_remote_copy(
                src_ref=here, dst_ref=here, send_sem=relay_send.at[slot], recv_sem=relay_recv.at[slot],
                device_id=toward(axis, step), device_id_type=MESH,
            )

        def arrive_line(step):
            here = spot((step, 0, 0), whole)
            pltpu.make_async_remote_copy(
                src_ref=here, dst_ref=here, send_sem=line_send.at[step], recv_sem=line_recv.at[step],
                device_id=toward(0, step), device_id_type=MESH,
            ).wait_recv()

        def arrive(part, offset):
            here = spot(offset, parts[part])
            slot = (part,) + offset
            pltpu.make_async_remote_copy(
                src_ref=here, dst_ref=here, send_sem=relay_send.at[slot], recv_sem=relay_recv.at[slot],
                device_id=toward(0, 1), device_id_type=MESH,
            ).wait_recv()

        sent = []

        def send(copy):
            copy.start()
            sent.append(copy)

        def spread(dz):
            for part in range(2):
                for axis in ((1, 2) if part == 0 else (2, 1)):
                    for step in range(1, grid[axis]):
                        send(relay(part, (dz, 0, 0), axis, step))

        for step in range(1, depth):
            send(line(step))
        spread(0)
        loads[2].wait()
        loads[3].wait()
        lax.fori_loop(0, chunks // 2, analyse, 0)
        for dz in range(1, depth):
            arrive_line(dz)
            spread(dz)
        lax.fori_loop(chunks // 2, chunks * 3 // 4, analyse, 0)
        for dz in range(depth):
            for step in range(1, height):
                arrive(0, (dz, step, 0))
                for last in range(1, breadth):
                    send(relay(0, (dz, step, 0), 2, last))
            for step in range(1, breadth):
                arrive(1, (dz, 0, step))
                for last in range(1, height):
                    send(relay(1, (dz, 0, step), 1, last))
        lax.fori_loop(chunks * 3 // 4, chunks, analyse, 0)
        for dz in range(depth):
            for dy in range(height):
                for dx in range(1, breadth):
                    arrive(0, (dz, dy, dx))
            for dx in range(breadth):
                for dy in range(1, height):
                    arrive(1, (dz, dy, dx))
        for copy in sent:
            copy.wait_send()

    @pl.when(section == 0)
    def _():
        gather(samples // 2)
        source = lax.broadcasted_iota(jnp.int32, (samples // 2, samples), 0)
        target = lax.broadcasted_iota(jnp.int32, (samples // 2, samples), 1)
        hold = jnp.where(source == target // 2, 1.0, 0.0).astype(jnp.bfloat16)
        for at in range(0, gathered.shape[0], 256):
            some = slice(at, at + 256)
            gathered[some, :] = dot(gathered[some, : samples // 2], hold).astype(jnp.bfloat16)

    @pl.when(section != 0)
    def _():
        gather(samples)

    for load in loads[4:]:
        load.wait()

    def swap(c):
        at = pl.ds(pl.multiple_of(c * CHUNK, CHUNK), CHUNK)
        return pltpu.make_async_remote_copy(
            src_ref=own.at[at],
            dst_ref=theirs.at[at],
            send_sem=swap_send.at[c],
            recv_sem=swap_recv.at[c],
            device_id={"sect": 1 - section},
            device_id_type=MESH,
        )

    def multiply(c):
        at = pl.ds(pl.multiple_of(c * CHUNK, CHUNK), CHUNK)
        value = dot(synthesis[at, :], gathered[...])
        own[at, :] = value.astype(jnp.bfloat16)
        for i in range(samples // LANES):
            kept[i, at, :] = value[:, i * LANES : (i + 1) * LANES]

    def emit(c):
        at = pl.ds(pl.multiple_of(c * CHUNK, CHUNK), CHUNK)
        to = pl.ds(pl.multiple_of(c * half, half), half)
        return (
            pltpu.make_async_copy(snr_out.at[at], snr_hbm.at[at], out_sems.at[0, c]),
            pltpu.make_async_copy(residual_out.at[to], residual_hbm.at[to], out_sems.at[1, c]),
        )

    def resolve(c):
        at = pl.ds(pl.multiple_of(c * CHUNK, CHUNK), CHUNK)
        to = pl.ds(pl.multiple_of(c * half, half), half)
        even, odd = pl.ds(0, half, stride=2), pl.ds(1, half, stride=2)
        for i in range(samples // LANES):
            full[i] = kept[i, at, :] + theirs[at, i * LANES : (i + 1) * LANES].astype(jnp.float32)
        xs_in, ys_in, high, low = [], [], [], []
        for i in range(samples // LANES):
            x, y = full[i, even, :], full[i, odd, :]
            xs_in.append(x.astype(jnp.bfloat16))
            ys_in.append(y.astype(jnp.bfloat16))
            power = x * x + y * y
            top = power.astype(jnp.bfloat16)
            high.append(top)
            low.append((power - top.astype(jnp.float32)).astype(jnp.bfloat16))
        xs_in, ys_in = jnp.concatenate(xs_in, axis=1), jnp.concatenate(ys_in, axis=1)
        spectrum = dot(jnp.concatenate([xs_in, ys_in], axis=0), forward[...])
        energy = dot(jnp.concatenate(high, axis=1), band[...])
        energy = energy + dot(jnp.concatenate(low, axis=1), band[...])
        ur, ui, vr, vi = [], [], [], []
        for i in range(tiles):
            cos = slice(i * LANES, (i + 1) * LANES)
            sin = slice((tiles + i) * LANES, (tiles + i + 1) * LANES)
            xc, yc = spectrum[:half, cos], spectrum[half:, cos]
            xs, ys = spectrum[:half, sin], spectrum[half:, sin]
            pr, pi = spectra[0, i, to, :], spectra[1, i, to, :]
            mr, mi = spectra[2, i, to, :], spectra[3, i, to, :]
            zpr, zpi, zmr, zmi = xc + ys, yc - xs, xc - ys, -xs - yc
            wpr, wpi = zpr * pr - zpi * pi, zpr * pi + zpi * pr
            wmr, wmi = zmr * mr - zmi * mi, zmr * mi + zmi * mr
            ur.append((wpr + wmr).astype(jnp.bfloat16))
            ui.append((wpi + wmi).astype(jnp.bfloat16))
            vr.append((wpi - wmi).astype(jnp.bfloat16))
            vi.append((wmr - wpr).astype(jnp.bfloat16))
        u = dot(jnp.concatenate(ur + ui, axis=1), inverse[...])
        v = dot(jnp.concatenate(vr + vi, axis=1), inverse[...])
        weight = weights[to, :]
        for i in range(share // LANES):
            columns = slice(i * LANES, (i + 1) * LANES)
            tile = section * (share // LANES) + i
            snr_out[at, columns] = full[tile].astype(jnp.bfloat16)
            x, y = full[tile, even, :], full[tile, odd, :]
            cross = x * u[:, columns] + y * v[:, columns]
            value = energy[:, columns] - 2.0 * cross + (x * x + y * y) * weight
            residual_out[to, columns] = value / (2.0 * length)
    ahead = min(2, chunks)

    def lead(c, carry):
        multiply(c)
        swap(c).start()
        return carry

    def both(c, carry):
        swap(c).wait()
        multiply(c + ahead)
        resolve(c)
        swap(c + ahead).start()
        for copy in emit(c):
            copy.start()
        return carry

    def trail(c, carry):
        swap(c).wait()
        resolve(c)
        for copy in emit(c):
            copy.start()
        return carry

    lax.fori_loop(0, ahead, lead, 0)
    lax.fori_loop(0, chunks - ahead, both, 0)
    lax.fori_loop(chunks - ahead, chunks, trail, 0)

    def finish(c, carry):
        for copy in emit(c):
            copy.wait()
        return carry

    lax.fori_loop(0, chunks, finish, 0)


def grid_of(mesh):
    tmpl = mesh.axis_names.index("tmpl")
    line = np.moveaxis(mesh.devices, tmpl, 0).reshape(mesh.shape["tmpl"], -1)[:, 0]
    spots = np.array([device.coords for device in line])[:, ::-1]
    spots = spots - spots.min(axis=0)
    grid = tuple(int(size) for size in spots.max(axis=0) + 1)
    if np.array_equal(spots @ [grid[1] * grid[2], grid[2], 1], np.arange(len(line))):
        return grid
    return (len(line), 1, 1)


def local(grid, strain, filters, synthesis, correlation):
    sections = lax.axis_size("sect")
    n = lax.axis_size("tmpl")
    block, taps = filters.shape[1:]
    samples = strain.shape[1] - taps + 1
    share = samples // sections
    rows = synthesis.shape[1]
    groups, _, length = correlation.shape
    forward, series, inverse, band = transforms(samples, share, sections, length)
    depth, spectrum = series.shape
    tiles = spectrum // (2 * LANES)
    chunks = rows // CHUNK
    hbm = pl.BlockSpec(memory_space=pl.ANY)
    return pl.pallas_call(
        functools.partial(kernel, length, grid),
        out_shape=(
            jax.ShapeDtypeStruct((rows, share), jnp.bfloat16),
            jax.ShapeDtypeStruct((groups, share), jnp.float32),
        ),
        in_specs=[pl.BlockSpec(memory_space=pltpu.HBM)] * 8,
        out_specs=(hbm, hbm),
        scratch_shapes=[
            pltpu.VMEM(strain.shape, jnp.bfloat16),
            pltpu.VMEM((block, taps), jnp.bfloat16),
            pltpu.VMEM((rows, n * block), jnp.bfloat16),
            pltpu.VMEM((depth, 2, groups), jnp.float32),
            pltpu.VMEM(forward.shape[1:], jnp.bfloat16),
            pltpu.VMEM(series.shape, jnp.bfloat16),
            pltpu.VMEM(inverse.shape[1:], jnp.bfloat16),
            pltpu.VMEM(band.shape[1:], jnp.bfloat16),
            pltpu.VMEM((n * block, samples), jnp.bfloat16),
            pltpu.VMEM((rows, samples), jnp.bfloat16),
            pltpu.VMEM((rows, samples), jnp.bfloat16),
            pltpu.VMEM((4, tiles, groups, LANES), jnp.float32),
            pltpu.VMEM((groups, LANES), jnp.float32),
            pltpu.VMEM((samples // LANES, rows, LANES), jnp.float32),
            pltpu.VMEM((samples // LANES, CHUNK, LANES), jnp.float32),
            pltpu.VMEM((rows, share), jnp.bfloat16),
            pltpu.VMEM((groups, share), jnp.float32),
            pltpu.SemaphoreType.DMA((8,)),
            pltpu.SemaphoreType.DMA((2, chunks)),
            pltpu.SemaphoreType.DMA((grid[0],)),
            pltpu.SemaphoreType.DMA((grid[0],)),
            pltpu.SemaphoreType.DMA((2,) + grid),
            pltpu.SemaphoreType.DMA((2,) + grid),
            pltpu.SemaphoreType.DMA((chunks,)),
            pltpu.SemaphoreType.DMA((chunks,)),
        ],
        compiler_params=pltpu.CompilerParams(
            collective_id=0, has_side_effects=True, vmem_limit_bytes=36 * 2**20
        ),
    )(
        strain, filters[0], synthesis, correlation.transpose(2, 1, 0),
        forward, series, inverse, band,
    )


def solution(mesh):
    placed = (
        P("sect", None),
        P("sect", "tmpl", None),
        P("sect", "tmpl", None),
        P("tmpl", None, None),
    )
    return jax.shard_map(
        functools.partial(local, grid_of(mesh)),
        mesh=mesh,
        in_specs=placed,
        out_specs=(P("tmpl", "sect"), P("tmpl", "sect")),
        check_vma=False,
    )
```

```python
import functools

import numpy as np
import jax
import jax.numpy as jnp
from jax import lax
from jax.experimental import pallas as pl
from jax.experimental.pallas import tpu as pltpu
from jax.sharding import PartitionSpec as P

LANES = 128
TAP_GROUP = 128
SUBLANES = 8
CHUNK = 256
MESH = pl.DeviceIdType.MESH


def transforms(samples, share, sections, length):
    centre = (length - 1) // 2
    freqs = -(-(share + length - 1) // (2 * LANES)) * LANES
    depth = -(-length // LANES) * LANES
    omega = np.pi * (np.arange(freqs) + 0.5) / freqs
    times = np.arange(samples)
    angle = times[:, None] * omega[None, :]
    forward = np.concatenate([np.cos(angle), np.sin(angle)], axis=1)
    first = np.arange(sections)[:, None] * share
    near = (times[None] >= first - centre) & (times[None] < first + share + length - 1 - centre)
    forward = np.where(near[:, :, None], forward[None], 0.0)
    lags = (np.arange(depth) - centre)[:, None] * omega[None, :]
    series = np.concatenate([np.cos(lags), np.sin(lags)], axis=1)
    series = np.where(np.arange(depth)[:, None] < length, series, 0.0)
    back = angle.reshape(sections, share, freqs).transpose(0, 2, 1)
    inverse = np.concatenate([np.cos(back), -np.sin(back)], axis=1) / (2 * freqs)
    reach = times[None, :, None] - (first + np.arange(share)[None])[:, None, :]
    band = (reach >= -centre) & (reach < length - centre)
    return tuple(np.asarray(x, jnp.bfloat16) for x in (forward, series, inverse, band))


def dot(a, b):
    return jnp.dot(a, b, preferred_element_type=jnp.float32)


def dot_rows(a, b):
    return lax.dot_general(a, b, (((0,), (0,)), ((), ())), preferred_element_type=jnp.float32)


def kernel(
    length, grid,
    strain_hbm, filters_hbm, synthesis_hbm, lags_hbm,
    forward_hbm, series_hbm, inverse_hbm, band_hbm,
    snr_hbm, residual_hbm,
    strain_ref, filters_ref, synthesis, lags, forward, series, inverse, band,
    gathered, own, theirs, spectra, weights, kept, full, snr_out, residual_out,
    in_sems, out_sems, line_send, line_recv, relay_send, relay_recv, swap_send, swap_recv,
):
    n = lax.axis_size("tmpl")
    me = lax.axis_index("tmpl")
    section = lax.axis_index("sect")
    block, samples = filters_ref.shape[0], gathered.shape[1]
    taps = filters_ref.shape[1]
    share = residual_out.shape[1]
    rows = synthesis.shape[0]
    chunks = rows // CHUNK
    half = CHUNK // 2
    tiles = spectra.shape[1]

    loads = [
        pltpu.make_async_copy(src, dst, in_sems.at[i])
        for i, (src, dst) in enumerate([
            (strain_hbm, strain_ref),
            (filters_hbm, filters_ref),
            (lags_hbm.at[:, 0], lags.at[0]),
            (lags_hbm.at[:, 1], lags.at[1]),
            (series_hbm, series),
            (synthesis_hbm.at[0], synthesis),
            (forward_hbm.at[section], forward),
            (inverse_hbm.at[section], inverse),
            (band_hbm.at[section], band),
        ])
    ]
    for load in loads:
        load.start()

    depth, height, breadth = grid
    place = (me // (height * breadth), me // breadth % height, me % breadth)

    def toward(axis, step):
        where = [lax.rem(p + step, size) if i == axis else p for i, (p, size) in enumerate(zip(place, grid))]
        return {"tmpl": (where[0] * height + where[1]) * breadth + where[2]}

    barrier = pltpu.get_barrier_semaphore()
    for axis in range(3):
        for step in range(1, grid[axis]):
            pl.semaphore_signal(barrier, inc=1, device_id=toward(axis, step), device_id_type=MESH)
    pl.semaphore_signal(barrier, inc=1, device_id={"sect": 1 - section}, device_id_type=MESH)
    loads[0].wait()
    loads[1].wait()
    signal = strain_ref[...].astype(jnp.float32)
    signal = jnp.concatenate([signal, jnp.zeros((1, -signal.shape[1] % LANES), jnp.float32)], axis=1)
    width = signal.shape[1]
    shifted = [signal] + [pltpu.roll(signal, width - i, 1) for i in range(1, SUBLANES)]
    shifted = jnp.concatenate(shifted, axis=0)
    hankel = [shifted] + [
        pltpu.roll(shifted, width - i, 1) for i in range(SUBLANES, TAP_GROUP, SUBLANES)
    ]
    hankel = jnp.concatenate(hankel, axis=0).astype(jnp.bfloat16)
    basis = jnp.zeros((block, samples), jnp.float32)
    for at in range(0, taps, TAP_GROUP):
        basis = basis + dot(filters_ref[:, at : at + TAP_GROUP], hankel[:, at : at + samples])
    mine = gathered.at[pl.ds(pl.multiple_of(me * block, block), block)]
    mine[...] = basis.astype(jnp.bfloat16)

    pl.semaphore_wait(barrier, sum(grid) - 3 + 1)

    def analyse(c, carry):
        at = pl.ds(pl.multiple_of(c * half, half), half)
        a, b = lags[0, :, at], lags[1, :, at]
        real = dot_rows(a.astype(jnp.bfloat16), series[pl.ds(0, length), :])
        imag = dot_rows(b.astype(jnp.bfloat16), series[pl.ds(0, length), :])
        power = a * a + b * b
        high = power.astype(jnp.bfloat16)
        low = (power - high.astype(jnp.float32)).astype(jnp.bfloat16)
        ones = jnp.ones((length, LANES), jnp.bfloat16)
        weights[at, :] = dot_rows(high, ones) + dot_rows(low, ones)
        for i in range(tiles):
            cos = slice(i * LANES, (i + 1) * LANES)
            sin = slice((tiles + i) * LANES, (tiles + i + 1) * LANES)
            ac, as_, bc, bs = real[:, cos], real[:, sin], imag[:, cos], imag[:, sin]
            spectra[0, i, at, :] = ac + bs
            spectra[1, i, at, :] = as_ - bc
            spectra[2, i, at, :] = ac - bs
            spectra[3, i, at, :] = as_ + bc
        return carry

    def gather(used):
        whole = pl.ds(0, used)
        parts = (pl.ds(0, used // 2), pl.ds(used // 2, used // 2))

        def spot(offset, columns):
            where = [lax.rem(p - o + size, size) for p, o, size in zip(place, offset, grid)]
            index = (where[0] * height + where[1]) * breadth + where[2]
            return gathered.at[pl.ds(pl.multiple_of(index * block, block), block), columns]

        def line(step):
            here = spot((0, 0, 0), whole)
            return pltpu.make_async_remote_copy(
                src_ref=here, dst_ref=here, send_sem=line_send.at[step], recv_sem=line_recv.at[step],
                device_id=toward(0, step), device_id_type=MESH,
            )

        def relay(part, offset, axis, step):
            here = spot(offset, parts[part])
            there = tuple(step if i == axis else o for i, o in enumerate(offset))
            slot = (part,) + there
            return pltpu.make_async_remote_copy(
                src_ref=here, dst_ref=here, send_sem=relay_send.at[slot], recv_sem=relay_recv.at[slot],
                device_id=toward(axis, step), device_id_type=MESH,
            )

        def arrive_line(step):
            here = spot((step, 0, 0), whole)
            pltpu.make_async_remote_copy(
                src_ref=here, dst_ref=here, send_sem=line_send.at[step], recv_sem=line_recv.at[step],
                device_id=toward(0, step), device_id_type=MESH,
            ).wait_recv()

        def arrive(part, offset):
            here = spot(offset, parts[part])
            slot = (part,) + offset
            pltpu.make_async_remote_copy(
                src_ref=here, dst_ref=here, send_sem=relay_send.at[slot], recv_sem=relay_recv.at[slot],
                device_id=toward(0, 1), device_id_type=MESH,
            ).wait_recv()

        sent = []

        def send(copy):
            copy.start()
            sent.append(copy)

        def spread(dz):
            for part in range(2):
                for axis in ((1, 2) if part == 0 else (2, 1)):
                    for step in range(1, grid[axis]):
                        send(relay(part, (dz, 0, 0), axis, step))

        for step in range(1, depth):
            send(line(step))
        spread(0)
        loads[2].wait()
        loads[3].wait()
        loads[4].wait()
        lax.fori_loop(0, chunks // 2, analyse, 0)
        for dz in range(1, depth):
            arrive_line(dz)
            spread(dz)
        lax.fori_loop(chunks // 2, chunks * 3 // 4, analyse, 0)
        for dz in range(depth):
            for step in range(1, height):
                arrive(0, (dz, step, 0))
                for last in range(1, breadth):
                    send(relay(0, (dz, step, 0), 2, last))
            for step in range(1, breadth):
                arrive(1, (dz, 0, step))
                for last in range(1, height):
                    send(relay(1, (dz, 0, step), 1, last))
        lax.fori_loop(chunks * 3 // 4, chunks, analyse, 0)
        for dz in range(depth):
            for dy in range(height):
                for dx in range(1, breadth):
                    arrive(0, (dz, dy, dx))
            for dx in range(breadth):
                for dy in range(1, height):
                    arrive(1, (dz, dy, dx))
        for copy in sent:
            copy.wait_send()

    @pl.when(section == 0)
    def _():
        gather(samples // 2)
        source = lax.broadcasted_iota(jnp.int32, (samples // 2, samples), 0)
        target = lax.broadcasted_iota(jnp.int32, (samples // 2, samples), 1)
        hold = jnp.where(source == target // 2, 1.0, 0.0).astype(jnp.bfloat16)
        for at in range(0, gathered.shape[0], 256):
            some = slice(at, at + 256)
            gathered[some, :] = dot(gathered[some, : samples // 2], hold).astype(jnp.bfloat16)

    @pl.when(section != 0)
    def _():
        gather(samples)

    for load in loads[5:]:
        load.wait()

    def swap(c):
        at = pl.ds(pl.multiple_of(c * CHUNK, CHUNK), CHUNK)
        return pltpu.make_async_remote_copy(
            src_ref=own.at[at],
            dst_ref=theirs.at[at],
            send_sem=swap_send.at[c],
            recv_sem=swap_recv.at[c],
            device_id={"sect": 1 - section},
            device_id_type=MESH,
        )

    def multiply(c):
        at = pl.ds(pl.multiple_of(c * CHUNK, CHUNK), CHUNK)
        value = dot(synthesis[at, :], gathered[...])
        own[at, :] = value.astype(jnp.bfloat16)
        for i in range(samples // LANES):
            kept[i, at, :] = value[:, i * LANES : (i + 1) * LANES]

    def emit(c):
        at = pl.ds(pl.multiple_of(c * CHUNK, CHUNK), CHUNK)
        to = pl.ds(pl.multiple_of(c * half, half), half)
        return (
            pltpu.make_async_copy(snr_out.at[at], snr_hbm.at[at], out_sems.at[0, c]),
            pltpu.make_async_copy(residual_out.at[to], residual_hbm.at[to], out_sems.at[1, c]),
        )

    def resolve(c):
        at = pl.ds(pl.multiple_of(c * CHUNK, CHUNK), CHUNK)
        to = pl.ds(pl.multiple_of(c * half, half), half)
        even, odd = pl.ds(0, half, stride=2), pl.ds(1, half, stride=2)
        for i in range(samples // LANES):
            full[i] = kept[i, at, :] + theirs[at, i * LANES : (i + 1) * LANES].astype(jnp.float32)
        xs_in, ys_in, high, low = [], [], [], []
        for i in range(samples // LANES):
            x, y = full[i, even, :], full[i, odd, :]
            xs_in.append(x.astype(jnp.bfloat16))
            ys_in.append(y.astype(jnp.bfloat16))
            power = x * x + y * y
            top = power.astype(jnp.bfloat16)
            high.append(top)
            low.append((power - top.astype(jnp.float32)).astype(jnp.bfloat16))
        xs_in, ys_in = jnp.concatenate(xs_in, axis=1), jnp.concatenate(ys_in, axis=1)
        spectrum = dot(jnp.concatenate([xs_in, ys_in], axis=0), forward[...])
        high, low = jnp.concatenate(high, axis=1), jnp.concatenate(low, axis=1)
        energy = dot(jnp.concatenate([high, low], axis=0), band[...])
        energy = energy[:half] + energy[half:]
        ur, ui, vr, vi = [], [], [], []
        for i in range(tiles):
            cos = slice(i * LANES, (i + 1) * LANES)
            sin = slice((tiles + i) * LANES, (tiles + i + 1) * LANES)
            xc, yc = spectrum[:half, cos], spectrum[half:, cos]
            xs, ys = spectrum[:half, sin], spectrum[half:, sin]
            pr, pi = spectra[0, i, to, :], spectra[1, i, to, :]
            mr, mi = spectra[2, i, to, :], spectra[3, i, to, :]
            zpr, zpi, zmr, zmi = xc + ys, yc - xs, xc - ys, -xs - yc
            wpr, wpi = zpr * pr - zpi * pi, zpr * pi + zpi * pr
            wmr, wmi = zmr * mr - zmi * mi, zmr * mi + zmi * mr
            ur.append((wpr + wmr).astype(jnp.bfloat16))
            ui.append((wpi + wmi).astype(jnp.bfloat16))
            vr.append((wpi - wmi).astype(jnp.bfloat16))
            vi.append((wmr - wpr).astype(jnp.bfloat16))
        turned = jnp.concatenate(
            [jnp.concatenate(ur + ui, axis=1), jnp.concatenate(vr + vi, axis=1)], axis=0
        )
        turned = dot(turned, inverse[...])
        u, v = turned[:half], turned[half:]
        weight = weights[to, :]
        for i in range(share // LANES):
            columns = slice(i * LANES, (i + 1) * LANES)
            tile = section * (share // LANES) + i
            snr_out[at, columns] = full[tile].astype(jnp.bfloat16)
            x, y = full[tile, even, :], full[tile, odd, :]
            cross = x * u[:, columns] + y * v[:, columns]
            value = energy[:, columns] - 2.0 * cross + (x * x + y * y) * weight
            residual_out[to, columns] = value / (2.0 * length)
    ahead = min(2, chunks)

    def lead(c, carry):
        multiply(c)
        swap(c).start()
        return carry

    def both(c, carry):
        swap(c).wait()
        multiply(c + ahead)
        resolve(c)
        swap(c + ahead).start()
        for copy in emit(c):
            copy.start()
        return carry

    def trail(c, carry):
        swap(c).wait()
        resolve(c)
        for copy in emit(c):
            copy.start()
        return carry

    lax.fori_loop(0, ahead, lead, 0)
    lax.fori_loop(0, chunks - ahead, both, 0)
    lax.fori_loop(chunks - ahead, chunks, trail, 0)

    def finish(c, carry):
        for copy in emit(c):
            copy.wait()
        return carry

    lax.fori_loop(0, chunks, finish, 0)


def grid_of(mesh):
    tmpl = mesh.axis_names.index("tmpl")
    line = np.moveaxis(mesh.devices, tmpl, 0).reshape(mesh.shape["tmpl"], -1)[:, 0]
    spots = np.array([device.coords for device in line])[:, ::-1]
    spots = spots - spots.min(axis=0)
    grid = tuple(int(size) for size in spots.max(axis=0) + 1)
    if np.array_equal(spots @ [grid[1] * grid[2], grid[2], 1], np.arange(len(line))):
        return grid
    return (len(line), 1, 1)


def local(grid, strain, filters, synthesis, correlation):
    sections = lax.axis_size("sect")
    n = lax.axis_size("tmpl")
    block, taps = filters.shape[1:]
    samples = strain.shape[1] - taps + 1
    share = samples // sections
    rows = synthesis.shape[1]
    groups, _, length = correlation.shape
    forward, series, inverse, band = transforms(samples, share, sections, length)
    depth, spectrum = series.shape
    tiles = spectrum // (2 * LANES)
    chunks = rows // CHUNK
    hbm = pl.BlockSpec(memory_space=pl.ANY)
    return pl.pallas_call(
        functools.partial(kernel, length, grid),
        out_shape=(
            jax.ShapeDtypeStruct((rows, share), jnp.bfloat16),
            jax.ShapeDtypeStruct((groups, share), jnp.float32),
        ),
        in_specs=[pl.BlockSpec(memory_space=pltpu.HBM)] * 8,
        out_specs=(hbm, hbm),
        scratch_shapes=[
            pltpu.VMEM(strain.shape, jnp.bfloat16),
            pltpu.VMEM((block, taps), jnp.bfloat16),
            pltpu.VMEM((rows, n * block), jnp.bfloat16),
            pltpu.VMEM((2, length, groups), jnp.float32),
            pltpu.VMEM(forward.shape[1:], jnp.bfloat16),
            pltpu.VMEM(series.shape, jnp.bfloat16),
            pltpu.VMEM(inverse.shape[1:], jnp.bfloat16),
            pltpu.VMEM(band.shape[1:], jnp.bfloat16),
            pltpu.VMEM((n * block, samples), jnp.bfloat16),
            pltpu.VMEM((rows, samples), jnp.bfloat16),
            pltpu.VMEM((rows, samples), jnp.bfloat16),
            pltpu.VMEM((4, tiles, groups, LANES), jnp.float32),
            pltpu.VMEM((groups, LANES), jnp.float32),
            pltpu.VMEM((samples // LANES, rows, LANES), jnp.float32),
            pltpu.VMEM((samples // LANES, CHUNK, LANES), jnp.float32),
            pltpu.VMEM((rows, share), jnp.bfloat16),
            pltpu.VMEM((groups, share), jnp.float32),
            pltpu.SemaphoreType.DMA((9,)),
            pltpu.SemaphoreType.DMA((2, chunks)),
            pltpu.SemaphoreType.DMA((grid[0],)),
            pltpu.SemaphoreType.DMA((grid[0],)),
            pltpu.SemaphoreType.DMA((2,) + grid),
            pltpu.SemaphoreType.DMA((2,) + grid),
            pltpu.SemaphoreType.DMA((chunks,)),
            pltpu.SemaphoreType.DMA((chunks,)),
        ],
        compiler_params=pltpu.CompilerParams(
            collective_id=0, has_side_effects=True, vmem_limit_bytes=56 * 2**20
        ),
    )(
        strain, filters[0], synthesis, correlation.transpose(2, 1, 0),
        forward, series, inverse, band,
    )


def solution(mesh):
    placed = (
        P("sect", None),
        P("sect", "tmpl", None),
        P("sect", "tmpl", None),
        P("tmpl", None, None),
    )
    return jax.shard_map(
        functools.partial(local, grid_of(mesh)),
        mesh=mesh,
        in_specs=placed,
        out_specs=(P("tmpl", "sect"), P("tmpl", "sect")),
        check_vma=False,
    )
```

```python
import functools

import numpy as np
import jax
import jax.numpy as jnp
from jax import lax
from jax.experimental import pallas as pl
from jax.experimental.pallas import tpu as pltpu
from jax.sharding import PartitionSpec as P

LANES = 128
TAP_GROUP = 128
SUBLANES = 8
CHUNK = 512
COPIES = 4
MESH = pl.DeviceIdType.MESH


def transforms(samples, share, sections, length):
    centre = (length - 1) // 2
    freqs = -(-(share + length - 1) // (2 * LANES)) * LANES
    depth = -(-length // LANES) * LANES
    omega = np.pi * (np.arange(freqs) + 0.5) / freqs
    times = np.arange(samples)
    angle = times[:, None] * omega[None, :]
    forward = np.concatenate([np.cos(angle), np.sin(angle)], axis=1)
    first = np.arange(sections)[:, None] * share
    near = (times[None] >= first - centre) & (times[None] < first + share + length - 1 - centre)
    forward = np.where(near[:, :, None], forward[None], 0.0)
    lags = (np.arange(depth) - centre)[:, None] * omega[None, :]
    series = np.concatenate([np.cos(lags), np.sin(lags)], axis=1)
    series = np.where(np.arange(depth)[:, None] < length, series, 0.0)
    back = angle.reshape(sections, share, freqs).transpose(0, 2, 1)
    inverse = np.concatenate([np.cos(back), -np.sin(back)], axis=1) / (2 * freqs)
    reach = times[None, :, None] - (first + np.arange(share)[None])[:, None, :]
    band = (reach >= -centre) & (reach < length - centre)
    return tuple(np.asarray(x, jnp.bfloat16) for x in (forward, series, inverse, band))


def dot(a, b):
    return jnp.dot(a, b, preferred_element_type=jnp.float32)


def dot_rows(a, b):
    return lax.dot_general(a, b, (((0,), (0,)), ((), ())), preferred_element_type=jnp.float32)


def kernel(
    length, grid,
    strain_hbm, filters_hbm, synthesis_hbm, lags_hbm,
    forward_hbm, series_hbm, inverse_hbm, band_hbm,
    snr_hbm, residual_hbm,
    strain_ref, filters_ref, synthesis, lags, forward, series, inverse, band,
    gathered, own, theirs, spectra, weights, kept, full, snr_out, residual_out,
    in_sems, out_sems, line_send, line_recv, relay_send, relay_recv, swap_send, swap_recv,
):
    n = lax.axis_size("tmpl")
    me = lax.axis_index("tmpl")
    section = lax.axis_index("sect")
    block, samples = filters_ref.shape[0], gathered.shape[1]
    taps = filters_ref.shape[1]
    share = residual_out.shape[1]
    rows = synthesis.shape[0]
    chunks = rows // CHUNK
    half = CHUNK // 2
    tiles = spectra.shape[1]

    loads = [
        pltpu.make_async_copy(src, dst, in_sems.at[i])
        for i, (src, dst) in enumerate([
            (strain_hbm, strain_ref),
            (filters_hbm, filters_ref),
            (lags_hbm.at[:, 0], lags.at[0]),
            (lags_hbm.at[:, 1], lags.at[1]),
            (series_hbm, series),
            (synthesis_hbm.at[0], synthesis),
            (forward_hbm.at[section], forward),
            (inverse_hbm.at[section], inverse),
            (band_hbm.at[section], band),
        ])
    ]
    for load in loads:
        load.start()

    depth, height, breadth = grid
    place = (me // (height * breadth), me // breadth % height, me % breadth)

    def toward(axis, step):
        where = [lax.rem(p + step, size) if i == axis else p for i, (p, size) in enumerate(zip(place, grid))]
        return {"tmpl": (where[0] * height + where[1]) * breadth + where[2]}

    barrier = pltpu.get_barrier_semaphore()
    for axis in range(3):
        for step in range(1, grid[axis]):
            pl.semaphore_signal(barrier, inc=1, device_id=toward(axis, step), device_id_type=MESH)
    pl.semaphore_signal(barrier, inc=1, device_id={"sect": 1 - section}, device_id_type=MESH)
    loads[0].wait()
    loads[1].wait()
    signal = strain_ref[...].astype(jnp.float32)
    signal = jnp.concatenate([signal, jnp.zeros((1, -signal.shape[1] % LANES), jnp.float32)], axis=1)
    width = signal.shape[1]
    shifted = [signal] + [pltpu.roll(signal, width - i, 1) for i in range(1, SUBLANES)]
    shifted = jnp.concatenate(shifted, axis=0)
    hankel = [shifted] + [
        pltpu.roll(shifted, width - i, 1) for i in range(SUBLANES, TAP_GROUP, SUBLANES)
    ]
    hankel = jnp.concatenate(hankel, axis=0).astype(jnp.bfloat16)
    basis = jnp.zeros((block, samples), jnp.float32)
    for at in range(0, taps, TAP_GROUP):
        basis = basis + dot(filters_ref[:, at : at + TAP_GROUP], hankel[:, at : at + samples])
    mine = gathered.at[pl.ds(pl.multiple_of(me * block, block), block)]
    mine[...] = basis.astype(jnp.bfloat16)

    pl.semaphore_wait(barrier, sum(grid) - 3 + 1)

    def analyse(c, carry):
        at = pl.ds(pl.multiple_of(c * half, half), half)
        a, b = lags[0, :, at], lags[1, :, at]
        real = dot_rows(a.astype(jnp.bfloat16), series[pl.ds(0, length), :])
        imag = dot_rows(b.astype(jnp.bfloat16), series[pl.ds(0, length), :])
        power = a * a + b * b
        high = power.astype(jnp.bfloat16)
        low = (power - high.astype(jnp.float32)).astype(jnp.bfloat16)
        ones = jnp.ones((length, LANES), jnp.bfloat16)
        weights[at, :] = dot_rows(high, ones) + dot_rows(low, ones)
        for i in range(tiles):
            cos = slice(i * LANES, (i + 1) * LANES)
            sin = slice((tiles + i) * LANES, (tiles + i + 1) * LANES)
            ac, as_, bc, bs = real[:, cos], real[:, sin], imag[:, cos], imag[:, sin]
            spectra[0, i, at, :] = ac + bs
            spectra[1, i, at, :] = as_ - bc
            spectra[2, i, at, :] = ac - bs
            spectra[3, i, at, :] = as_ + bc
        return carry

    def gather(used):
        whole = pl.ds(0, used)
        parts = (pl.ds(0, used // 2), pl.ds(used // 2, used // 2))

        def spot(offset, columns):
            where = [lax.rem(p - o + size, size) for p, o, size in zip(place, offset, grid)]
            index = (where[0] * height + where[1]) * breadth + where[2]
            return gathered.at[pl.ds(pl.multiple_of(index * block, block), block), columns]

        def line(step):
            here = spot((0, 0, 0), whole)
            return pltpu.make_async_remote_copy(
                src_ref=here, dst_ref=here, send_sem=line_send.at[step], recv_sem=line_recv.at[step],
                device_id=toward(0, step), device_id_type=MESH,
            )

        def relay(part, offset, axis, step):
            here = spot(offset, parts[part])
            there = tuple(step if i == axis else o for i, o in enumerate(offset))
            slot = (part,) + there
            return pltpu.make_async_remote_copy(
                src_ref=here, dst_ref=here, send_sem=relay_send.at[slot], recv_sem=relay_recv.at[slot],
                device_id=toward(axis, step), device_id_type=MESH,
            )

        def arrive_line(step):
            here = spot((step, 0, 0), whole)
            pltpu.make_async_remote_copy(
                src_ref=here, dst_ref=here, send_sem=line_send.at[step], recv_sem=line_recv.at[step],
                device_id=toward(0, step), device_id_type=MESH,
            ).wait_recv()

        def arrive(part, offset):
            here = spot(offset, parts[part])
            slot = (part,) + offset
            pltpu.make_async_remote_copy(
                src_ref=here, dst_ref=here, send_sem=relay_send.at[slot], recv_sem=relay_recv.at[slot],
                device_id=toward(0, 1), device_id_type=MESH,
            ).wait_recv()

        sent = []

        def send(copy):
            copy.start()
            sent.append(copy)

        def spread(dz):
            for part in range(2):
                for axis in ((1, 2) if part == 0 else (2, 1)):
                    for step in range(1, grid[axis]):
                        send(relay(part, (dz, 0, 0), axis, step))

        for step in range(1, depth):
            send(line(step))
        spread(0)
        loads[2].wait()
        loads[3].wait()
        loads[4].wait()
        lax.fori_loop(0, chunks // 2, analyse, 0)
        for dz in range(1, depth):
            arrive_line(dz)
            spread(dz)
        lax.fori_loop(chunks // 2, chunks * 3 // 4, analyse, 0)
        for dz in range(depth):
            for step in range(1, height):
                arrive(0, (dz, step, 0))
                for last in range(1, breadth):
                    send(relay(0, (dz, step, 0), 2, last))
            for step in range(1, breadth):
                arrive(1, (dz, 0, step))
                for last in range(1, height):
                    send(relay(1, (dz, 0, step), 1, last))
        lax.fori_loop(chunks * 3 // 4, chunks, analyse, 0)
        for dz in range(depth):
            for dy in range(height):
                for dx in range(1, breadth):
                    arrive(0, (dz, dy, dx))
            for dx in range(breadth):
                for dy in range(1, height):
                    arrive(1, (dz, dy, dx))
        for copy in sent:
            copy.wait_send()

    @pl.when(section == 0)
    def _():
        gather(samples // 2)
        source = lax.broadcasted_iota(jnp.int32, (samples // 2, samples), 0)
        target = lax.broadcasted_iota(jnp.int32, (samples // 2, samples), 1)
        hold = jnp.where(source == target // 2, 1.0, 0.0).astype(jnp.bfloat16)
        for at in range(0, gathered.shape[0], 256):
            some = slice(at, at + 256)
            gathered[some, :] = dot(gathered[some, : samples // 2], hold).astype(jnp.bfloat16)

    @pl.when(section != 0)
    def _():
        gather(samples)

    for load in loads[5:]:
        load.wait()

    def swap(c):
        at = pl.ds(pl.multiple_of(c * CHUNK, CHUNK), CHUNK)
        return pltpu.make_async_remote_copy(
            src_ref=own.at[at],
            dst_ref=theirs.at[at],
            send_sem=swap_send.at[c],
            recv_sem=swap_recv.at[c],
            device_id={"sect": 1 - section},
            device_id_type=MESH,
        )

    def multiply(c):
        at = pl.ds(pl.multiple_of(c * CHUNK, CHUNK), CHUNK)
        value = dot(synthesis[at, :], gathered[...])
        own[at, :] = value.astype(jnp.bfloat16)
        for i in range(samples // LANES):
            kept[i, at, :] = value[:, i * LANES : (i + 1) * LANES]

    def emit(c):
        at = pl.ds(pl.multiple_of(c * CHUNK, CHUNK), CHUNK)
        to = pl.ds(pl.multiple_of(c * half, half), half)
        return (
            pltpu.make_async_copy(snr_out.at[at], snr_hbm.at[at], out_sems.at[0, c]),
            pltpu.make_async_copy(residual_out.at[to], residual_hbm.at[to], out_sems.at[1, c]),
        )

    def resolve(c):
        at = pl.ds(pl.multiple_of(c * CHUNK, CHUNK), CHUNK)
        to = pl.ds(pl.multiple_of(c * half, half), half)
        even, odd = pl.ds(0, half, stride=2), pl.ds(1, half, stride=2)
        for i in range(samples // LANES):
            full[i] = kept[i, at, :] + theirs[at, i * LANES : (i + 1) * LANES].astype(jnp.float32)
        xs_in, ys_in, high, low = [], [], [], []
        for i in range(samples // LANES):
            x, y = full[i, even, :], full[i, odd, :]
            xs_in.append(x.astype(jnp.bfloat16))
            ys_in.append(y.astype(jnp.bfloat16))
            power = x * x + y * y
            top = power.astype(jnp.bfloat16)
            high.append(top)
            low.append((power - top.astype(jnp.float32)).astype(jnp.bfloat16))
        xs_in, ys_in = jnp.concatenate(xs_in, axis=1), jnp.concatenate(ys_in, axis=1)
        spectrum = dot(jnp.concatenate([xs_in, ys_in], axis=0), forward[...])
        high, low = jnp.concatenate(high, axis=1), jnp.concatenate(low, axis=1)
        energy = dot(jnp.concatenate([high, low], axis=0), band[...])
        energy = energy[:half] + energy[half:]
        ur, ui, vr, vi = [], [], [], []
        for i in range(tiles):
            cos = slice(i * LANES, (i + 1) * LANES)
            sin = slice((tiles + i) * LANES, (tiles + i + 1) * LANES)
            xc, yc = spectrum[:half, cos], spectrum[half:, cos]
            xs, ys = spectrum[:half, sin], spectrum[half:, sin]
            pr, pi = spectra[0, i, to, :], spectra[1, i, to, :]
            mr, mi = spectra[2, i, to, :], spectra[3, i, to, :]
            zpr, zpi, zmr, zmi = xc + ys, yc - xs, xc - ys, -xs - yc
            wpr, wpi = zpr * pr - zpi * pi, zpr * pi + zpi * pr
            wmr, wmi = zmr * mr - zmi * mi, zmr * mi + zmi * mr
            ur.append((wpr + wmr).astype(jnp.bfloat16))
            ui.append((wpi + wmi).astype(jnp.bfloat16))
            vr.append((wpi - wmi).astype(jnp.bfloat16))
            vi.append((wmr - wpr).astype(jnp.bfloat16))
        turned = jnp.concatenate(
            [jnp.concatenate(ur + ui, axis=1), jnp.concatenate(vr + vi, axis=1)], axis=0
        )
        turned = dot(turned, inverse[...])
        u, v = turned[:half], turned[half:]
        weight = weights[to, :]
        for i in range(share // LANES):
            columns = slice(i * LANES, (i + 1) * LANES)
            tile = section * (share // LANES) + i
            snr_out[at, columns] = full[tile].astype(jnp.bfloat16)
            x, y = full[tile, even, :], full[tile, odd, :]
            cross = x * u[:, columns] + y * v[:, columns]
            value = energy[:, columns] - 2.0 * cross + (x * x + y * y) * weight
            residual_out[to, columns] = value / (2.0 * length)
    ahead = min(2, chunks)

    def lead(c, carry):
        multiply(c)
        swap(c).start()
        return carry

    def both(c, carry):
        swap(c).wait()
        multiply(c + ahead)
        resolve(c)
        swap(c + ahead).start()
        for copy in emit(c):
            copy.start()
        return carry

    def trail(c, carry):
        swap(c).wait()
        resolve(c)
        for copy in emit(c):
            copy.start()
        return carry

    lax.fori_loop(0, ahead, lead, 0)
    lax.fori_loop(0, chunks - ahead, both, 0)
    lax.fori_loop(chunks - ahead, chunks, trail, 0)

    def finish(c, carry):
        for copy in emit(c):
            copy.wait()
        return carry

    lax.fori_loop(0, chunks, finish, 0)


def grid_of(mesh):
    tmpl = mesh.axis_names.index("tmpl")
    line = np.moveaxis(mesh.devices, tmpl, 0).reshape(mesh.shape["tmpl"], -1)[:, 0]
    spots = np.array([device.coords for device in line])[:, ::-1]
    spots = spots - spots.min(axis=0)
    grid = tuple(int(size) for size in spots.max(axis=0) + 1)
    if np.array_equal(spots @ [grid[1] * grid[2], grid[2], 1], np.arange(len(line))):
        return grid
    return (len(line), 1, 1)


def local(grid, strain, filters, synthesis, correlation):
    sections = lax.axis_size("sect")
    n = lax.axis_size("tmpl")
    block, taps = filters.shape[1:]
    samples = strain.shape[1] - taps + 1
    share = samples // sections
    rows = synthesis.shape[1]
    groups, _, length = correlation.shape
    forward, series, inverse, band = transforms(samples, share, sections, length)
    depth, spectrum = series.shape
    tiles = spectrum // (2 * LANES)
    chunks = rows // CHUNK
    hbm = pl.BlockSpec(memory_space=pl.ANY)
    results = pl.pallas_call(
        functools.partial(kernel, length, grid),
        out_shape=(
            jax.ShapeDtypeStruct((rows, share), jnp.bfloat16),
            jax.ShapeDtypeStruct((groups, share), jnp.float32),
        ),
        in_specs=[pl.BlockSpec(memory_space=pltpu.HBM)] * 8,
        out_specs=(hbm, hbm),
        scratch_shapes=[
            pltpu.VMEM(strain.shape, jnp.bfloat16),
            pltpu.VMEM((block, taps), jnp.bfloat16),
            pltpu.VMEM((rows, n * block), jnp.bfloat16),
            pltpu.VMEM((2, length, groups), jnp.float32),
            pltpu.VMEM(forward.shape[1:], jnp.bfloat16),
            pltpu.VMEM(series.shape, jnp.bfloat16),
            pltpu.VMEM(inverse.shape[1:], jnp.bfloat16),
            pltpu.VMEM(band.shape[1:], jnp.bfloat16),
            pltpu.VMEM((n * block, samples), jnp.bfloat16),
            pltpu.VMEM((rows, samples), jnp.bfloat16),
            pltpu.VMEM((rows, samples), jnp.bfloat16),
            pltpu.VMEM((4, tiles, groups, LANES), jnp.float32),
            pltpu.VMEM((groups, LANES), jnp.float32),
            pltpu.VMEM((samples // LANES, rows, LANES), jnp.float32),
            pltpu.VMEM((samples // LANES, CHUNK, LANES), jnp.float32),
            pltpu.VMEM((rows, share), jnp.bfloat16),
            pltpu.VMEM((groups, share), jnp.float32),
            pltpu.SemaphoreType.DMA((9,)),
            pltpu.SemaphoreType.DMA((2, chunks)),
            pltpu.SemaphoreType.DMA((grid[0],)),
            pltpu.SemaphoreType.DMA((grid[0],)),
            pltpu.SemaphoreType.DMA((2,) + grid),
            pltpu.SemaphoreType.DMA((2,) + grid),
            pltpu.SemaphoreType.DMA((chunks,)),
            pltpu.SemaphoreType.DMA((chunks,)),
        ],
        compiler_params=pltpu.CompilerParams(
            collective_id=0, has_side_effects=True, vmem_limit_bytes=56 * 2**20
        ),
    )(
        strain, filters[0], synthesis, correlation.transpose(2, 1, 0),
        forward, series, inverse, band,
    )
    return pl.pallas_call(
        hand_over,
        out_shape=tuple(jax.ShapeDtypeStruct(x.shape, x.dtype) for x in results),
        in_specs=[hbm, hbm],
        out_specs=(hbm, hbm),
        scratch_shapes=[pltpu.SemaphoreType.DMA((2, COPIES))],
        compiler_params=pltpu.CompilerParams(vmem_limit_bytes=56 * 2**20),
    )(*results)


def hand_over(snr_in, residual_in, snr_out, residual_out, sems):
    copies = []
    for k, (source, target) in enumerate([(snr_in, snr_out), (residual_in, residual_out)]):
        part = source.shape[0] // COPIES
        for i in range(COPIES):
            at = pl.ds(i * part, part)
            copies.append(pltpu.make_async_copy(source.at[at], target.at[at], sems.at[k, i]))
    for copy in copies:
        copy.start()
    for copy in copies:
        copy.wait()


def solution(mesh):
    placed = (
        P("sect", None),
        P("sect", "tmpl", None),
        P("sect", "tmpl", None),
        P("tmpl", None, None),
    )
    return jax.shard_map(
        functools.partial(local, grid_of(mesh)),
        mesh=mesh,
        in_specs=placed,
        out_specs=(P("tmpl", "sect"), P("tmpl", "sect")),
        check_vma=False,
    )
```

```python
import functools

import numpy as np
import jax
import jax.numpy as jnp
from jax import lax
from jax.experimental import pallas as pl
from jax.experimental.pallas import tpu as pltpu
from jax.sharding import PartitionSpec as P

LANES = 128
TAP_GROUP = 128
SUBLANES = 8
CHUNK = 512
COPIES = 4
MESH = pl.DeviceIdType.MESH


def transforms(samples, share, sections, length):
    centre = (length - 1) // 2
    freqs = -(-(share + length - 1) // (2 * LANES)) * LANES
    depth = -(-length // LANES) * LANES
    omega = np.pi * (np.arange(freqs) + 0.5) / freqs
    times = np.arange(samples)
    angle = times[:, None] * omega[None, :]
    forward = np.concatenate([np.cos(angle), np.sin(angle)], axis=1)
    first = np.arange(sections)[:, None] * share
    near = (times[None] >= first - centre) & (times[None] < first + share + length - 1 - centre)
    forward = np.where(near[:, :, None], forward[None], 0.0)
    lags = (np.arange(depth) - centre)[:, None] * omega[None, :]
    series = np.concatenate([np.cos(lags), np.sin(lags)], axis=1)
    series = np.where(np.arange(depth)[:, None] < length, series, 0.0)
    back = angle.reshape(sections, share, freqs).transpose(0, 2, 1)
    inverse = np.concatenate([np.cos(back), -np.sin(back)], axis=1) / (2 * freqs)
    reach = times[None, :, None] - (first + np.arange(share)[None])[:, None, :]
    band = (reach >= -centre) & (reach < length - centre)
    return tuple(np.asarray(x, jnp.bfloat16) for x in (forward, series, inverse, band))


def dot(a, b):
    return jnp.dot(a, b, preferred_element_type=jnp.float32)


def dot_rows(a, b):
    return lax.dot_general(a, b, (((0,), (0,)), ((), ())), preferred_element_type=jnp.float32)


def kernel(
    length, grid,
    strain_hbm, filters_hbm, synthesis_hbm, lags_hbm,
    forward_hbm, series_hbm, inverse_hbm, band_hbm,
    snr_hbm, residual_hbm,
    strain_ref, filters_ref, synthesis, lags, forward, series, inverse, band,
    gathered, own, theirs, spectra, weights, kept, full, snr_out, residual_out,
    in_sems, out_sems, line_send, line_recv, relay_send, relay_recv, swap_send, swap_recv,
):
    n = lax.axis_size("tmpl")
    me = lax.axis_index("tmpl")
    section = lax.axis_index("sect")
    block, samples = filters_ref.shape[0], gathered.shape[1]
    taps = filters_ref.shape[1]
    share = residual_out.shape[1]
    rows = synthesis.shape[0]
    chunks = rows // CHUNK
    half = CHUNK // 2
    tiles = spectra.shape[1]

    loads = [
        pltpu.make_async_copy(src, dst, in_sems.at[i])
        for i, (src, dst) in enumerate([
            (strain_hbm, strain_ref),
            (filters_hbm, filters_ref),
            (lags_hbm.at[:, 0], lags.at[0]),
            (lags_hbm.at[:, 1], lags.at[1]),
            (series_hbm, series),
            (synthesis_hbm.at[0], synthesis),
            (forward_hbm.at[section], forward),
            (inverse_hbm.at[section], inverse),
            (band_hbm.at[section], band),
        ])
    ]
    for load in loads:
        load.start()

    depth, height, breadth = grid
    place = (me // (height * breadth), me // breadth % height, me % breadth)

    def toward(axis, step):
        where = [lax.rem(p + step, size) if i == axis else p for i, (p, size) in enumerate(zip(place, grid))]
        return {"tmpl": (where[0] * height + where[1]) * breadth + where[2]}

    barrier = pltpu.get_barrier_semaphore()
    for axis in range(3):
        for step in range(1, grid[axis]):
            pl.semaphore_signal(barrier, inc=1, device_id=toward(axis, step), device_id_type=MESH)
    pl.semaphore_signal(barrier, inc=1, device_id={"sect": 1 - section}, device_id_type=MESH)
    loads[0].wait()
    loads[1].wait()
    signal = strain_ref[...].astype(jnp.float32)
    signal = jnp.concatenate([signal, jnp.zeros((1, -signal.shape[1] % LANES), jnp.float32)], axis=1)
    width = signal.shape[1]
    shifted = [signal] + [pltpu.roll(signal, width - i, 1) for i in range(1, SUBLANES)]
    shifted = jnp.concatenate(shifted, axis=0)
    hankel = [shifted] + [
        pltpu.roll(shifted, width - i, 1) for i in range(SUBLANES, TAP_GROUP, SUBLANES)
    ]
    hankel = jnp.concatenate(hankel, axis=0).astype(jnp.bfloat16)
    basis = jnp.zeros((block, samples), jnp.float32)
    for at in range(0, taps, TAP_GROUP):
        basis = basis + dot(filters_ref[:, at : at + TAP_GROUP], hankel[:, at : at + samples])
    mine = gathered.at[pl.ds(pl.multiple_of(me * block, block), block)]
    mine[...] = basis.astype(jnp.bfloat16)

    pl.semaphore_wait(barrier, sum(grid) - 3 + 1)

    def analyse(c, carry):
        at = pl.ds(pl.multiple_of(c * half, half), half)
        a, b = lags[0, :, at], lags[1, :, at]
        real = dot_rows(a.astype(jnp.bfloat16), series[pl.ds(0, length), :])
        imag = dot_rows(b.astype(jnp.bfloat16), series[pl.ds(0, length), :])
        power = a * a + b * b
        high = power.astype(jnp.bfloat16)
        low = (power - high.astype(jnp.float32)).astype(jnp.bfloat16)
        ones = jnp.ones((length, LANES), jnp.bfloat16)
        weights[at, :] = dot_rows(high, ones) + dot_rows(low, ones)
        for i in range(tiles):
            cos = slice(i * LANES, (i + 1) * LANES)
            sin = slice((tiles + i) * LANES, (tiles + i + 1) * LANES)
            ac, as_, bc, bs = real[:, cos], real[:, sin], imag[:, cos], imag[:, sin]
            spectra[0, i, at, :] = ac + bs
            spectra[1, i, at, :] = as_ - bc
            spectra[2, i, at, :] = ac - bs
            spectra[3, i, at, :] = as_ + bc
        return carry

    def gather(used):
        whole = pl.ds(0, used)
        parts = (pl.ds(0, used // 2), pl.ds(used // 2, used // 2))

        def spot(offset, columns):
            where = [lax.rem(p - o + size, size) for p, o, size in zip(place, offset, grid)]
            index = (where[0] * height + where[1]) * breadth + where[2]
            return gathered.at[pl.ds(pl.multiple_of(index * block, block), block), columns]

        def line(step):
            here = spot((0, 0, 0), whole)
            return pltpu.make_async_remote_copy(
                src_ref=here, dst_ref=here, send_sem=line_send.at[step], recv_sem=line_recv.at[step],
                device_id=toward(0, step), device_id_type=MESH,
            )

        def relay(part, offset, axis, step):
            here = spot(offset, parts[part])
            there = tuple(step if i == axis else o for i, o in enumerate(offset))
            slot = (part,) + there
            return pltpu.make_async_remote_copy(
                src_ref=here, dst_ref=here, send_sem=relay_send.at[slot], recv_sem=relay_recv.at[slot],
                device_id=toward(axis, step), device_id_type=MESH,
            )

        def arrive_line(step):
            here = spot((step, 0, 0), whole)
            pltpu.make_async_remote_copy(
                src_ref=here, dst_ref=here, send_sem=line_send.at[step], recv_sem=line_recv.at[step],
                device_id=toward(0, step), device_id_type=MESH,
            ).wait_recv()

        def arrive(part, offset):
            here = spot(offset, parts[part])
            slot = (part,) + offset
            pltpu.make_async_remote_copy(
                src_ref=here, dst_ref=here, send_sem=relay_send.at[slot], recv_sem=relay_recv.at[slot],
                device_id=toward(0, 1), device_id_type=MESH,
            ).wait_recv()

        sent = []

        def send(copy):
            copy.start()
            sent.append(copy)

        def spread(dz):
            for part in range(2):
                for axis in ((1, 2) if part == 0 else (2, 1)):
                    for step in range(1, grid[axis]):
                        send(relay(part, (dz, 0, 0), axis, step))

        for step in range(1, depth):
            send(line(step))
        spread(0)
        loads[2].wait()
        loads[3].wait()
        loads[4].wait()
        lax.fori_loop(0, chunks // 2, analyse, 0)
        for dz in range(1, depth):
            arrive_line(dz)
            spread(dz)
        lax.fori_loop(chunks // 2, chunks * 3 // 4, analyse, 0)
        for dz in range(depth):
            for step in range(1, height):
                arrive(0, (dz, step, 0))
                for last in range(1, breadth):
                    send(relay(0, (dz, step, 0), 2, last))
            for step in range(1, breadth):
                arrive(1, (dz, 0, step))
                for last in range(1, height):
                    send(relay(1, (dz, 0, step), 1, last))
        lax.fori_loop(chunks * 3 // 4, chunks, analyse, 0)
        for dz in range(depth):
            for dy in range(height):
                for dx in range(1, breadth):
                    arrive(0, (dz, dy, dx))
            for dx in range(breadth):
                for dy in range(1, height):
                    arrive(1, (dz, dy, dx))
        for copy in sent:
            copy.wait_send()

    @pl.when(section == 0)
    def _():
        gather(samples // 2)
        source = lax.broadcasted_iota(jnp.int32, (samples // 2, samples), 0)
        target = lax.broadcasted_iota(jnp.int32, (samples // 2, samples), 1)
        hold = jnp.where(source == target // 2, 1.0, 0.0).astype(jnp.bfloat16)
        for at in range(0, gathered.shape[0], 256):
            some = slice(at, at + 256)
            gathered[some, :] = dot(gathered[some, : samples // 2], hold).astype(jnp.bfloat16)

    @pl.when(section != 0)
    def _():
        gather(samples)

    for load in loads[5:]:
        load.wait()

    def swap(c):
        at = pl.ds(pl.multiple_of(c * CHUNK, CHUNK), CHUNK)
        return pltpu.make_async_remote_copy(
            src_ref=own.at[at],
            dst_ref=theirs.at[at],
            send_sem=swap_send.at[c],
            recv_sem=swap_recv.at[c],
            device_id={"sect": 1 - section},
            device_id_type=MESH,
        )

    def multiply(c):
        at = pl.ds(pl.multiple_of(c * CHUNK, CHUNK), CHUNK)
        value = dot(synthesis[at, :], gathered[...])
        own[at, :] = value.astype(jnp.bfloat16)
        for i in range(samples // LANES):
            kept[i, at, :] = value[:, i * LANES : (i + 1) * LANES]

    def emit(c):
        at = pl.ds(pl.multiple_of(c * CHUNK, CHUNK), CHUNK)
        to = pl.ds(pl.multiple_of(c * half, half), half)
        return (
            pltpu.make_async_copy(snr_out.at[at], snr_hbm.at[at], out_sems.at[0, c]),
            pltpu.make_async_copy(residual_out.at[to], residual_hbm.at[to], out_sems.at[1, c]),
        )

    def resolve(c):
        at = pl.ds(pl.multiple_of(c * CHUNK, CHUNK), CHUNK)
        to = pl.ds(pl.multiple_of(c * half, half), half)
        even, odd = pl.ds(0, half, stride=2), pl.ds(1, half, stride=2)
        for i in range(samples // LANES):
            full[i] = kept[i, at, :] + theirs[at, i * LANES : (i + 1) * LANES].astype(jnp.float32)
        xs_in, ys_in, high, low = [], [], [], []
        for i in range(samples // LANES):
            x, y = full[i, even, :], full[i, odd, :]
            xs_in.append(x.astype(jnp.bfloat16))
            ys_in.append(y.astype(jnp.bfloat16))
            power = x * x + y * y
            top = power.astype(jnp.bfloat16)
            high.append(top)
            low.append((power - top.astype(jnp.float32)).astype(jnp.bfloat16))
        xs_in, ys_in = jnp.concatenate(xs_in, axis=1), jnp.concatenate(ys_in, axis=1)
        spectrum = dot(jnp.concatenate([xs_in, ys_in], axis=0), forward[...])
        high, low = jnp.concatenate(high, axis=1), jnp.concatenate(low, axis=1)
        energy = dot(jnp.concatenate([high, low], axis=0), band[...])
        energy = energy[:half] + energy[half:]
        ur, ui, vr, vi = [], [], [], []
        for i in range(tiles):
            cos = slice(i * LANES, (i + 1) * LANES)
            sin = slice((tiles + i) * LANES, (tiles + i + 1) * LANES)
            xc, yc = spectrum[:half, cos], spectrum[half:, cos]
            xs, ys = spectrum[:half, sin], spectrum[half:, sin]
            pr, pi = spectra[0, i, to, :], spectra[1, i, to, :]
            mr, mi = spectra[2, i, to, :], spectra[3, i, to, :]
            zpr, zpi, zmr, zmi = xc + ys, yc - xs, xc - ys, -xs - yc
            wpr, wpi = zpr * pr - zpi * pi, zpr * pi + zpi * pr
            wmr, wmi = zmr * mr - zmi * mi, zmr * mi + zmi * mr
            ur.append((wpr + wmr).astype(jnp.bfloat16))
            ui.append((wpi + wmi).astype(jnp.bfloat16))
            vr.append((wpi - wmi).astype(jnp.bfloat16))
            vi.append((wmr - wpr).astype(jnp.bfloat16))
        turned = jnp.concatenate(
            [jnp.concatenate(ur + ui, axis=1), jnp.concatenate(vr + vi, axis=1)], axis=0
        )
        turned = dot(turned, inverse[...])
        u, v = turned[:half], turned[half:]
        weight = weights[to, :]
        for i in range(share // LANES):
            columns = slice(i * LANES, (i + 1) * LANES)
            tile = section * (share // LANES) + i
            snr_out[at, columns] = full[tile].astype(jnp.bfloat16)
            x, y = full[tile, even, :], full[tile, odd, :]
            cross = x * u[:, columns] + y * v[:, columns]
            value = energy[:, columns] - 2.0 * cross + (x * x + y * y) * weight
            residual_out[to, columns] = value / (2.0 * length)
    ahead = min(2, chunks)

    def lead(c, carry):
        multiply(c)
        swap(c).start()
        return carry

    def both(c, carry):
        swap(c).wait()
        multiply(c + ahead)
        resolve(c)
        swap(c + ahead).start()
        for copy in emit(c):
            copy.start()
        return carry

    def trail(c, carry):
        swap(c).wait()
        resolve(c)
        for copy in emit(c):
            copy.start()
        return carry

    lax.fori_loop(0, ahead, lead, 0)
    lax.fori_loop(0, chunks - ahead, both, 0)
    lax.fori_loop(chunks - ahead, chunks, trail, 0)

    def finish(c, carry):
        for copy in emit(c):
            copy.wait()
        return carry

    lax.fori_loop(0, chunks, finish, 0)


def grid_of(mesh):
    tmpl = mesh.axis_names.index("tmpl")
    line = np.moveaxis(mesh.devices, tmpl, 0).reshape(mesh.shape["tmpl"], -1)[:, 0]
    spots = np.array([device.coords for device in line])[:, ::-1]
    spots = spots - spots.min(axis=0)
    grid = tuple(int(size) for size in spots.max(axis=0) + 1)
    if np.array_equal(spots @ [grid[1] * grid[2], grid[2], 1], np.arange(len(line))):
        return grid
    return (len(line), 1, 1)


def local(grid, strain, filters, synthesis, correlation):
    sections = lax.axis_size("sect")
    n = lax.axis_size("tmpl")
    block, taps = filters.shape[1:]
    samples = strain.shape[1] - taps + 1
    share = samples // sections
    rows = synthesis.shape[1]
    groups, _, length = correlation.shape
    forward, series, inverse, band = transforms(samples, share, sections, length)
    depth, spectrum = series.shape
    tiles = spectrum // (2 * LANES)
    chunks = rows // CHUNK
    hbm = pl.BlockSpec(memory_space=pl.ANY)
    results = pl.pallas_call(
        functools.partial(kernel, length, grid),
        out_shape=(
            jax.ShapeDtypeStruct((rows, share), jnp.bfloat16),
            jax.ShapeDtypeStruct((groups, share), jnp.float32),
        ),
        in_specs=[pl.BlockSpec(memory_space=pltpu.HBM)] * 8,
        out_specs=(hbm, hbm),
        scratch_shapes=[
            pltpu.VMEM(strain.shape, jnp.bfloat16),
            pltpu.VMEM((block, taps), jnp.bfloat16),
            pltpu.VMEM((rows, n * block), jnp.bfloat16),
            pltpu.VMEM((2, length, groups), jnp.float32),
            pltpu.VMEM(forward.shape[1:], jnp.bfloat16),
            pltpu.VMEM(series.shape, jnp.bfloat16),
            pltpu.VMEM(inverse.shape[1:], jnp.bfloat16),
            pltpu.VMEM(band.shape[1:], jnp.bfloat16),
            pltpu.VMEM((n * block, samples), jnp.bfloat16),
            pltpu.VMEM((rows, samples), jnp.bfloat16),
            pltpu.VMEM((rows, samples), jnp.bfloat16),
            pltpu.VMEM((4, tiles, groups, LANES), jnp.float32),
            pltpu.VMEM((groups, LANES), jnp.float32),
            pltpu.VMEM((samples // LANES, rows, LANES), jnp.float32),
            pltpu.VMEM((samples // LANES, CHUNK, LANES), jnp.float32),
            pltpu.VMEM((rows, share), jnp.bfloat16),
            pltpu.VMEM((groups, share), jnp.float32),
            pltpu.SemaphoreType.DMA((9,)),
            pltpu.SemaphoreType.DMA((2, chunks)),
            pltpu.SemaphoreType.DMA((grid[0],)),
            pltpu.SemaphoreType.DMA((grid[0],)),
            pltpu.SemaphoreType.DMA((2,) + grid),
            pltpu.SemaphoreType.DMA((2,) + grid),
            pltpu.SemaphoreType.DMA((chunks,)),
            pltpu.SemaphoreType.DMA((chunks,)),
        ],
        compiler_params=pltpu.CompilerParams(
            collective_id=0, has_side_effects=True, vmem_limit_bytes=56 * 2**20
        ),
    )(
        strain, filters[0], synthesis, correlation.transpose(2, 1, 0),
        forward, series, inverse, band,
    )
    return pl.pallas_call(
        hand_over,
        out_shape=tuple(jax.ShapeDtypeStruct(x.shape, x.dtype) for x in results),
        in_specs=[hbm, hbm],
        out_specs=(hbm, hbm),
        scratch_shapes=[pltpu.VMEM(x.shape, x.dtype) for x in results]
        + [pltpu.SemaphoreType.DMA((2, COPIES))] * 2,
        compiler_params=pltpu.CompilerParams(vmem_limit_bytes=56 * 2**20),
    )(*results)


def hand_over(snr_in, residual_in, snr_out, residual_out, snr, residual, into, out):
    arrive, leave = [], []
    for k, (source, held, target) in enumerate(
        [(snr_in, snr, snr_out), (residual_in, residual, residual_out)]
    ):
        part = source.shape[0] // COPIES
        for i in range(COPIES):
            at = pl.ds(i * part, part)
            arrive.append(pltpu.make_async_copy(source.at[at], held.at[at], into.at[k, i]))
            leave.append(pltpu.make_async_copy(held.at[at], target.at[at], out.at[k, i]))
    for copy in arrive:
        copy.start()
    for first, second in zip(arrive, leave):
        first.wait()
        second.start()
    for copy in leave:
        copy.wait()


def solution(mesh):
    placed = (
        P("sect", None),
        P("sect", "tmpl", None),
        P("sect", "tmpl", None),
        P("tmpl", None, None),
    )
    return jax.shard_map(
        functools.partial(local, grid_of(mesh)),
        mesh=mesh,
        in_specs=placed,
        out_specs=(P("tmpl", "sect"), P("tmpl", "sect")),
        check_vma=False,
    )
```
